128 devices in a mesh: prompt: 4 (over x), response: 16 (over y_lo, z, core), tensor: 2 (over y_hi).
Axes of the slice: x: 4, y: 4 (y_hi: 2, y_lo: 2; y = y_hi * 2 + y_lo), z: 4, core: 2. Of those that a mesh axis runs over, the one named last changes fastest.
Arguments:
- queries: bfloat16 [4, 2048, 8192], P('prompt', 'response', 'tensor'), may hold values from -30 to 30
- keys: bfloat16 [4, 2048, 1024], P('prompt', 'response', 'tensor'), may hold values from -6 to 6
- values: bfloat16 [4, 2048, 1024], P('prompt', 'response', 'tensor'), may hold values from -36 to 36
- prefix_keys: bfloat16 [4, 2048, 1024], P('prompt', ('response', 'tensor')), may hold values from -6 to 6
- prefix_values: bfloat16 [4, 2048, 1024], P('prompt', ('response', 'tensor')), may hold values from -36 to 36
- lengths: int32 [4, 16], P('prompt', 'response'), may hold values from 1 to 128, as said below
- out_grad: bfloat16 [4, 2048, 8192], P('prompt', 'response', 'tensor'), may hold values from -36 to 36
Outputs:
- output: bfloat16 [4, 2048, 8192], P('prompt', 'response', 'tensor')
- query_grad: bfloat16 [4, 2048, 8192], P('prompt', 'response', 'tensor')
- key_grad: bfloat16 [4, 2048, 1024], P('prompt', 'response', 'tensor')
- value_grad: bfloat16 [4, 2048, 1024], P('prompt', 'response', 'tensor')
- prefix_key_grad: bfloat16 [4, 2048, 1024], P('prompt', ('response', 'tensor'))
- prefix_value_grad: bfloat16 [4, 2048, 1024], P('prompt', ('response', 'tensor'))
The draws below stay inside these ranges and needn't reach their ends.
Inputs may be any that keep to these rules, and one draw needn't show every extreme that they name: `lengths`: number of live tokens of response r of prompt p; they fill its first slots.
All inputs are finite; a program needn't handle non-finite values.
Results may differ from the reference program's by a relative error of at most 0.023.
Values may be sent and summed in bfloat16 or wider, within the bound.
A program may use at most 192 MiB of HBM per device.

```python
import math
import jax
import jax.numpy as jnp
from jax import lax

KVH = 8
HD = 128
GROUP = 8
ROWS_DEV = 128
PROMPTS = 4
RESPONSES = 16
PREFIX = 2048
RESP_ROWS = 2048


def draw_queries(key, part):
    key = jax.random.fold_in(key, 11)
    drawn = jnp.clip(jax.random.normal(key, (PROMPTS, RESP_ROWS, GROUP * KVH * HD), jnp.float32), -6.0, 6.0)
    return drawn.astype(jnp.bfloat16)


def draw_prefix_keys(key, part):
    key = jax.random.fold_in(key, 13)
    drawn = jnp.clip(jax.random.normal(key, (PROMPTS, PREFIX, KVH * HD), jnp.float32), -6.0, 6.0)
    return drawn.astype(jnp.bfloat16)


def draw_lengths(key, part):
    key = jax.random.fold_in(key, 17)
    first_key, second_key, third_key = jax.random.split(key, 3)
    prompt_ids = jnp.arange(PROMPTS, dtype=jnp.int32)[:, None]
    response_ids = jnp.arange(RESPONSES, dtype=jnp.int32)[None, :]
    lower = jnp.maximum(1, ROWS_DEV * (prompt_ids + 1) // (2 * PROMPTS))
    upper = ROWS_DEV * (prompt_ids + 1) // PROMPTS + 1
    drawn = jax.random.randint(first_key, (PROMPTS, RESPONSES), lower, upper)
    shortest = jax.random.randint(third_key, (), 0, RESPONSES)
    shortrow = (prompt_ids == 0) & (response_ids == shortest)
    drawn = jnp.where(shortrow, 1, drawn)
    chosen = jax.random.randint(second_key, (), 0, RESPONSES)
    fullrow = (prompt_ids == PROMPTS - 1) & (response_ids == chosen)
    return jnp.where(fullrow, ROWS_DEV, drawn).astype(jnp.int32)


def steps_of(stream_key, dims, shards, smallest, top_value):
    def one(dim, parts):
        steps = jax.random.uniform(jax.random.fold_in(jax.random.fold_in(stream_key, 6), dim), (parts,), jnp.float32, smallest / len(shards), top_value / len(shards))
        return jnp.repeat(jnp.exp(steps), dims[dim] // parts).reshape((-1,) + (1,) * (len(dims) - dim - 1))

    loudness = one(*shards[0])
    for cut in shards[1:]:
        loudness = loudness * one(*cut)
    return loudness


def noise(key, dims, spread, bound, cuts=(), held_as=jnp.bfloat16):
    level = steps_of(key, dims, cuts, -0.22, 0.18) if cuts else 1.0
    values = jax.random.normal(key, dims, jnp.float32) * spread * level
    return jnp.minimum(jnp.maximum(values, -bound), bound).astype(held_as)


def setup_inputs(seed: int = 0) -> dict:
    key_of = jax.random.split(jax.random.key(seed), 8)
    queries = draw_queries(jax.random.fold_in(key_of[7], 71), 0)
    keys = noise(key_of[1], (PROMPTS, RESP_ROWS, KVH * HD), 1.0, 6.0, ((0, 4), (1, 16), (2, 2)))
    values = noise(key_of[2], (PROMPTS, RESP_ROWS, KVH * HD), 6.0, 36.0, ((0, 4), (1, 16), (2, 2)))
    prefix_keys = draw_prefix_keys(jax.random.fold_in(key_of[7], 71), 0)
    prefix_values = noise(key_of[4], (PROMPTS, PREFIX, KVH * HD), 6.0, 36.0, ((0, 4), (1, 32)))
    lengths = draw_lengths(jax.random.fold_in(key_of[7], 71), 0)
    out_grad = noise(key_of[6], (PROMPTS, RESP_ROWS, GROUP * KVH * HD), 6.0, 36.0, ((0, 4), (1, 16), (2, 2)))
    return {"queries": queries, "keys": keys, "values": values, "prefix_keys": prefix_keys, "prefix_values": prefix_values, "lengths": lengths, "out_grad": out_grad}


def attend_head(head_queries, own_keys, own_values, pre_keys, pre_values, live_rows, scaled_grad):
    row_count = head_queries.shape[0]
    prefix_len = pre_keys.shape[0]
    all_keys = jnp.concatenate([pre_keys, own_keys], axis=0).astype(jnp.float32)
    all_values = jnp.concatenate([pre_values, own_values], axis=0).astype(jnp.float32)
    query_rows = head_queries.astype(jnp.float32)
    grad_rows = scaled_grad.astype(jnp.float32)
    factor = 1.0 / math.sqrt(head_queries.shape[2])
    scores = jnp.einsum('rgd,kd->grk', query_rows, all_keys) * factor
    row_pos = jnp.arange(row_count, dtype=jnp.int32)[:, None]
    key_pos = jnp.arange(prefix_len + row_count, dtype=jnp.int32)[None, :] - prefix_len
    allowed = key_pos <= row_pos
    scores = jnp.where(allowed[None], scores, -1e+30)
    row_max = lax.optimization_barrier(jnp.max(scores, axis=2, keepdims=True))
    exponent = jnp.exp(scores - row_max)
    probs = exponent / lax.optimization_barrier(jnp.sum(exponent, axis=2, keepdims=True))
    rounded = probs.astype(jnp.bfloat16)
    rounded_wide = rounded.astype(jnp.float32)
    attended = jnp.einsum('grk,kd->rgd', rounded_wide, all_values)
    output = (attended * live_rows[:, None, None]).astype(jnp.bfloat16)
    grad_probs = jnp.einsum('rgd,kd->grk', grad_rows, all_values)
    centre = lax.optimization_barrier(jnp.sum(grad_rows * attended, axis=2))
    score_grad = (probs * (grad_probs - jnp.transpose(centre)[:, :, None]) * factor).astype(jnp.bfloat16)
    score_wide = score_grad.astype(jnp.float32)
    query_grad = jnp.einsum('grk,kd->rgd', score_wide, all_keys)
    key_grad = jnp.einsum('grk,rgd->kd', score_wide, query_rows)
    value_grad = jnp.einsum('grk,rgd->kd', rounded_wide, grad_rows)
    return (output, query_grad, key_grad[:prefix_len], key_grad[prefix_len:], value_grad[:prefix_len], value_grad[prefix_len:])

def response_rows(resp_queries, resp_keys, resp_values, pre_keys, pre_values, length, resp_grad, weight):
    row_count = resp_queries.shape[0]
    live_rows = (jnp.arange(row_count, dtype=jnp.int32) < length).astype(jnp.float32)
    scaled = (resp_grad.astype(jnp.float32) * live_rows[:, None] * weight).astype(jnp.bfloat16)
    head_count = resp_keys.shape[1] // HD
    outputs, query_grads, key_grads, value_grads, pre_kgs, pre_vgs = ([], [], [], [], [], [])
    for kv_head in range(head_count):
        qstart = kv_head * GROUP * HD
        kstart = kv_head * HD
        block_queries = resp_queries[:, qstart:qstart + GROUP * HD].reshape(row_count, GROUP, HD)
        block_grad = scaled[:, qstart:qstart + GROUP * HD].reshape(row_count, GROUP, HD)
        results = attend_head(block_queries, resp_keys[:, kstart:kstart + HD], resp_values[:, kstart:kstart + HD], pre_keys[:, kstart:kstart + HD], pre_values[:, kstart:kstart + HD], live_rows, block_grad)
        outputs.append(results[0].reshape(row_count, GROUP * HD))
        query_grads.append(results[1].reshape(row_count, GROUP * HD))
        pre_kgs.append(results[2])
        key_grads.append(results[3])
        pre_vgs.append(results[4])
        value_grads.append(results[5])
    return (jnp.concatenate(outputs, axis=1), jnp.concatenate(query_grads, axis=1).astype(jnp.bfloat16), jnp.concatenate(key_grads, axis=1).astype(jnp.bfloat16), jnp.concatenate(value_grads, axis=1).astype(jnp.bfloat16), jnp.concatenate(pre_kgs, axis=1), jnp.concatenate(pre_vgs, axis=1))

def by_response(array):
    return array.reshape(RESPONSES, ROWS_DEV, array.shape[1])

def reference(queries, keys, values, prefix_keys, prefix_values, lengths, out_grad):
    live_total = jnp.sum(lengths.astype(jnp.float32))
    weight = PROMPTS * RESPONSES * ROWS_DEV / live_total

    def per_prompt(prompt_items):
        p_queries, p_keys, p_values, p_pre_keys, p_pre_values, p_lengths, p_grad = prompt_items

        def per_response(running, response_items):
            r_queries, r_keys, r_values, r_length, r_grad = response_items
            results = response_rows(r_queries, r_keys, r_values, p_pre_keys, p_pre_values, r_length, r_grad, weight)
            return ((running[0] + results[4], running[1] + results[5]), (results[0], results[1], results[2], results[3]))
        zero_grads = jnp.zeros(p_pre_keys.shape, jnp.float32)
        prefix_sums, results = lax.scan(per_response, (zero_grads, zero_grads), (by_response(p_queries), by_response(p_keys), by_response(p_values), p_lengths, by_response(p_grad)))
        merged = [part_rows.reshape(RESPONSES * ROWS_DEV, part_rows.shape[2]) for part_rows in results]
        return (merged[0], merged[1], merged[2], merged[3], prefix_sums[0].astype(jnp.bfloat16), prefix_sums[1].astype(jnp.bfloat16))
    stacked = lax.map(per_prompt, (queries, keys, values, prefix_keys, prefix_values, lengths, out_grad))
    return (stacked[0], stacked[1], stacked[2], stacked[3], stacked[4], stacked[5])
```

```python
import math

import jax
import jax.numpy as jnp
from jax import lax
from jax.experimental import pallas as pl
from jax.experimental.pallas import tpu as pltpu
from jax.sharding import PartitionSpec as P

HD = 128
GROUP = 8
ROWS = 128
LOCAL = 64
BLOCK = 512
NBLOCK = 4
CHUNK = 1024
HALF = 512
HEADS = 2
QCOLS = HEADS * GROUP * HD
KCOLS = HEADS * HD
FACTOR = 1.0 / math.sqrt(HD)
EXP2 = math.log2(math.e) * FACTOR
MESH = pl.DeviceIdType.MESH
f32 = jnp.float32
bf16 = jnp.bfloat16


def dot(a, b):
    return jnp.dot(a, b, preferred_element_type=f32)


def kernel(
    q_in, k_in, v_in, pk_in, pv_in, len_in, do_in,
    o_out, dq_out, dk_out, dv_out, pkg_out, pvg_out,
    pk, pv, qin, din, kown, vown, kbuf, vbuf, lens, lsum,
    qt, qn, dot_, don, vt, kt, kot, vot, e, eo, mx, acc, cen, dq,
    ost, dqst, dkst, dvst, dks, dvs, rk, rv,
    load_sem, pair_send, pair_recv, own_sem, k_send, v_send, k_recv, v_recv,
    len_send, len_recv, dk_send, dv_send, dk_recv, dv_recv, out_send, out_recv, out_sem,
):
    prompt = lax.axis_index("prompt")
    resp = lax.axis_index("response")
    y_hi = lax.axis_index("tensor")
    core = lax.rem(resp, 2)
    z = lax.rem(resp // 2, 4)
    y_lo = resp // 8
    y = y_hi * 2 + y_lo
    other = 1 - core

    def at(zz, yy, cc):
        return {"response": lax.rem(yy, 2) * 8 + zz * 2 + cc, "tensor": yy // 2}

    def along_x(pp):
        return {"prompt": pp}

    sibling = {"response": resp + 1 - 2 * core}
    my_q = pl.ds(pl.multiple_of(core * QCOLS, QCOLS), QCOLS)
    its_q = pl.ds(pl.multiple_of(other * QCOLS, QCOLS), QCOLS)
    my_k = pl.ds(pl.multiple_of(core * KCOLS, KCOLS), KCOLS)
    its_k = pl.ds(pl.multiple_of(other * KCOLS, KCOLS), KCOLS)

    loads = [
        pltpu.make_async_copy(pk_in.at[0], pk, load_sem.at[0]),
        pltpu.make_async_copy(pv_in.at[0], pv, load_sem.at[1]),
        pltpu.make_async_copy(q_in.at[0, :, my_q], qin.at[0], load_sem.at[2]),
        pltpu.make_async_copy(do_in.at[0, :, my_q], din.at[0], load_sem.at[3]),
        pltpu.make_async_copy(k_in.at[0, :, my_k], kown.at[0], load_sem.at[4]),
        pltpu.make_async_copy(v_in.at[0, :, my_k], vown.at[0], load_sem.at[5]),
    ]
    for copy in loads:
        copy.start()

    barrier = pltpu.get_barrier_semaphore()

    @pl.loop(1, 32)
    def _(j):
        pl.semaphore_signal(
            barrier,
            inc=1,
            device_id=at(
                lax.rem(z + j // 8, 4),
                lax.rem(y + lax.rem(j // 2, 4), 4),
                lax.rem(core + lax.rem(j, 2), 2),
            ),
            device_id_type=MESH,
        )

    for step in range(1, 4):
        pl.semaphore_signal(
            barrier, inc=1, device_id=along_x(lax.rem(prompt + step, 4)), device_id_type=MESH
        )
    pl.semaphore_wait(barrier, 34)

    def send(src, dst, send_sem, recv_sem, device):
        return pltpu.make_async_remote_copy(
            src_ref=src,
            dst_ref=dst,
            send_sem=send_sem,
            recv_sem=recv_sem,
            device_id=device,
            device_id_type=MESH,
        )

    lens[0, prompt] = jnp.full((8, 128), len_in[0, 0], jnp.int32).astype(f32)
    pair = [
        send(lens.at[0, prompt], lsum.at[1], pair_send.at[0], pair_recv.at[0], sibling),
        send(q_in.at[0, :, its_q], qin.at[1], pair_send.at[1], pair_recv.at[1], sibling),
        send(k_in.at[0, :, its_k], kown.at[1], pair_send.at[2], pair_recv.at[2], sibling),
        send(do_in.at[0, :, its_q], din.at[1], pair_send.at[3], pair_recv.at[3], sibling),
        send(v_in.at[0, :, its_k], vown.at[1], pair_send.at[4], pair_recv.at[4], sibling),
    ]
    lsum[0] = lens[0, prompt]
    pair[0].start()
    pair[1].start()
    pair[2].start()

    my_row = pl.multiple_of((y * 2 + core) * LOCAL, LOCAL)
    order = ((0, 0), (1, 1), (2, 3), (3, 2))

    def push(shard, buf, send_sems, recv_sems):
        for block, dist in order:
            to_z = lax.rem(z + 4 - dist, 4)
            for n in range(8):
                if block == 0 and n == 0:
                    continue
                to_y = lax.rem(y + n // 2, 4)
                to_core = lax.rem(core + n % 2, 2)
                cols = pl.multiple_of(((to_y // 2) * 2 + to_core) * KCOLS, KCOLS)
                send(
                    shard.at[:, pl.ds(cols, KCOLS)],
                    buf.at[pl.ds(block * BLOCK + my_row, LOCAL)],
                    send_sems.at[block * 8 + n],
                    recv_sems.at[block],
                    at(to_z, to_y, to_core),
                ).start()

    def push_done(shard, buf, send_sems, recv_sems):
        @pl.loop(1, 32)
        def _(n):
            send(
                shard.at[:, pl.ds(0, KCOLS)],
                buf.at[pl.ds(0, LOCAL)],
                send_sems.at[n],
                recv_sems.at[0],
                sibling,
            ).wait_send()

    mine = pl.ds(pl.multiple_of((y_hi * 2 + core) * KCOLS, KCOLS), KCOLS)
    loads[0].wait()
    push(pk, kbuf, k_send, k_recv)
    pltpu.make_async_copy(pk.at[:, mine], kbuf.at[pl.ds(my_row, LOCAL)], k_recv.at[0]).start()
    pair[3].start()
    pair[4].start()
    loads[1].wait()
    push(pv, vbuf, v_send, v_recv)
    pltpu.make_async_copy(pv.at[:, mine], vbuf.at[pl.ds(my_row, LOCAL)], v_recv.at[0]).start()

    def x_copy(step):
        return send(
            lens.at[0, prompt], lens.at[0, prompt], len_send.at[0, step - 1],
            len_recv.at[0, step - 1], along_x(lax.rem(prompt + step, 4)),
        )

    def z_copy(step):
        return send(
            lens.at[1, z], lens.at[1, z], len_send.at[1, step - 1],
            len_recv.at[1, step - 1], at(lax.rem(z + step, 4), y, core),
        )

    rest = y_lo * 2 + core

    def rest_copy(step):
        slot = lax.rem(rest + step, 4)
        return send(
            lens.at[2, rest], lens.at[2, rest], len_send.at[2, step - 1],
            len_recv.at[2, step - 1], at(z, y_hi * 2 + slot // 2, lax.rem(slot, 2)),
        )

    for step in range(1, 4):
        x_copy(step).start()

    slot_row = lax.broadcasted_iota(jnp.int32, (ROWS, HD), 0).astype(f32)

    def stage_q(s):
        for h in range(HEADS):
            for g in range(GROUP):
                cols = pl.ds((h * GROUP + g) * HD, HD)
                block = qin[s, :, cols]
                qn[h, s, g * ROWS : (g + 1) * ROWS, :] = block
                qt[h, s, :, g * ROWS : (g + 1) * ROWS] = block.T

    def stage_do(s):
        live = slot_row < lsum[s, 0:1, :]
        for h in range(HEADS):
            for g in range(GROUP):
                cols = pl.ds((h * GROUP + g) * HD, HD)
                block = jnp.where(live, din[s, :, cols].astype(f32), 0.0).astype(bf16)
                dot_[h, s, :, g * ROWS : (g + 1) * ROWS] = block.T

    def stage_own(s):
        for h in range(HEADS):
            cols = pl.ds(h * HD, HD)
            kot[h, s] = kown[s, :, cols].T
            vot[h, s, 0:HD] = vown[s, :, cols].T
            vot[h, s, HD : HD + 16] = jnp.ones((16, ROWS), bf16)

    allowed = lax.broadcasted_iota(jnp.int32, (ROWS, HALF), 0) <= lax.rem(
        lax.broadcasted_iota(jnp.int32, (ROWS, HALF), 1), ROWS
    )

    def own_scores(h, s, part):
        scores = dot(kown[s, :, pl.ds(h * HD, HD)], qt[h, s, :, part * HALF : (part + 1) * HALF])
        return jnp.where(allowed, scores, -1e30)

    def own_max(s):
        for h in range(HEADS):
            for part in range(2):
                cols = pl.ds(part * HALF, HALF)
                mx[h, s, :, cols] = jnp.max(
                    own_scores(h, s, part).reshape(ROWS // 8, 8, HALF), axis=0
                )

    loads[2].wait()
    loads[4].wait()
    stage_q(0)
    own_max(0)
    loads[3].wait()
    stage_do(0)
    loads[5].wait()
    stage_own(0)
    for h in range(HEADS):
        vt[h, HD : HD + 16] = jnp.ones((16, NBLOCK * BLOCK), bf16)
    pair[0].wait_recv()
    pair[1].wait_recv()
    pair[2].wait_recv()
    stage_q(1)
    own_max(1)

    @pl.loop(0, NBLOCK)
    def _(j):
        base = pl.multiple_of(j * BLOCK, BLOCK)
        keys = kbuf.at[pl.ds(base, BLOCK)]
        pltpu.make_async_copy(keys, keys, k_recv.at[j]).wait()
        for h in range(HEADS):
            cols = pl.ds(h * HD, HD)
            for n in range(BLOCK // 128):
                kt[h, :, pl.ds(base + n * 128, 128)] = kbuf[pl.ds(base + n * 128, 128), cols].T
            for s in range(2):
                for part in range(2):
                    rows = pl.ds(part * HALF, HALF)
                    scores = dot(kbuf[pl.ds(base, BLOCK), cols], qt[h, s, :, rows])
                    mx[h, s, :, rows] = jnp.maximum(
                        mx[h, s, :, rows],
                        jnp.max(scores.reshape(BLOCK // 8, 8, HALF), axis=0),
                    )

    for step in range(1, 4):
        x_copy(step).wait_recv()
    lens[1, z] = lens[0, 0] + lens[0, 1] + lens[0, 2] + lens[0, 3]
    for step in range(1, 4):
        z_copy(step).start()

    pair[3].wait_recv()
    pair[4].wait_recv()
    stage_do(1)
    stage_own(1)

    for h in range(HEADS):
        for s in range(2):
            top = jnp.max(mx[h, s], axis=0, keepdims=True) * EXP2
            mx[h, s] = jnp.broadcast_to(top, (8, CHUNK))
            for part in range(2):
                rows = pl.ds(part * HALF, HALF)
                power = jnp.exp2(own_scores(h, s, part) * EXP2 - mx[h, s, 0:1, rows]).astype(bf16)
                eo[h, s, :, rows] = power
                acc[h, s, :, rows] = dot(vot[h, s], power)

    @pl.loop(0, NBLOCK)
    def _(j):
        base = pl.multiple_of(j * BLOCK, BLOCK)
        vals = vbuf.at[pl.ds(base, BLOCK)]
        pltpu.make_async_copy(vals, vals, v_recv.at[j]).wait()
        for h in range(HEADS):
            cols = pl.ds(h * HD, HD)
            for n in range(BLOCK // 128):
                vt[h, 0:HD, pl.ds(base + n * 128, 128)] = vbuf[
                    pl.ds(base + n * 128, 128), cols
                ].T
            for s in range(2):
                for part in range(2):
                    rows = pl.ds(part * HALF, HALF)
                    scores = dot(kbuf[pl.ds(base, BLOCK), cols], qt[h, s, :, rows])
                    power = jnp.exp2(scores * EXP2 - mx[h, s, 0:1, rows]).astype(bf16)
                    e[h, j, s, :, rows] = power
                    acc[h, s, :, rows] += dot(vt[h, :, pl.ds(base, BLOCK)], power)

    for step in range(1, 4):
        z_copy(step).wait_recv()
    lens[2, rest] = lens[1, 0] + lens[1, 1] + lens[1, 2] + lens[1, 3]
    for step in range(1, 4):
        rest_copy(step).start()

    def put(src, out, dst_cols, n):
        return (
            pltpu.make_async_copy(src.at[0], out.at[0, :, dst_cols], out_sem.at[n]),
            send(src.at[1], out.at[0, :, dst_cols], out_send.at[n], out_recv.at[n], sibling),
        )

    for s in range(2):
        live = slot_row < lsum[s, 0:1, :]
        for h in range(HEADS):
            inv = 1.0 / acc[h, s, HD : HD + 1, :]
            attended = acc[h, s, 0:HD, :] * inv
            cotangent = dot_[h, s].astype(f32)
            cen[h, s] = jnp.sum(attended * cotangent, axis=0, keepdims=True) * inv
            scaled = (cotangent * inv).astype(bf16)
            dot_[h, s] = scaled
            for g in range(GROUP):
                rows = slice(g * ROWS, (g + 1) * ROWS)
                don[h, s, rows, :] = scaled[:, rows].T
                ost[s, :, pl.ds((h * GROUP + g) * HD, HD)] = jnp.where(
                    live, attended[:, rows].T, 0.0
                ).astype(bf16)
    o_copies = put(ost, o_out, my_q, 0)
    o_copies[0].start()
    o_copies[1].start()

    for step in range(1, 4):
        rest_copy(step).wait_recv()
    total = lens[2, 0] + lens[2, 1] + lens[2, 2] + lens[2, 3]
    weight = (4.0 * 16.0 * ROWS) / total[0:1, :]

    for h in range(HEADS):
        cols = pl.ds(h * HD, HD)
        for s in range(2):
            power = eo[h, s]
            grad = dot(vown[s, :, cols], dot_[h, s])
            score = (power.astype(f32) * (grad - cen[h, s])).astype(bf16)
            dvst[s, :, cols] = (dot(power, don[h, s]) * weight).astype(bf16)
            dkst[s, :, cols] = (dot(score, qn[h, s]) * (weight * FACTOR)).astype(bf16)
            dq[h, s] = dot(kot[h, s], score)
    dk_copies = put(dkst, dk_out, my_k, 1)
    dv_copies = put(dvst, dv_out, my_k, 2)
    for copy in dk_copies + dv_copies:
        copy.start()

    slot = (y_hi * 2 + core) * 8 + z * 2 + y_lo

    def grad_copy(j, n, stage, landing, send_sems, recv_sem):
        dist = j + (j // 2) * (5 - 2 * j)
        row = pl.multiple_of(j * BLOCK + n * LOCAL, LOCAL)
        return send(
            stage.at[pl.ds(row, LOCAL)],
            landing.at[slot],
            send_sems.at[j * 8 + n],
            recv_sem,
            at(lax.rem(z + dist, 4), n // 2, lax.rem(n, 2)),
        )

    def self_copy(stage, landing, recv_sem):
        return pltpu.make_async_copy(stage.at[pl.ds(my_row, LOCAL)], landing.at[slot], recv_sem)

    me = y * 2 + core

    @pl.loop(0, NBLOCK)
    def _(back):
        j = NBLOCK - 1 - back
        base = pl.multiple_of(j * BLOCK, BLOCK)
        for h in range(HEADS):
            cols = pl.ds(h * HD, HD)
            dv_part = None
            dk_part = None
            for s in range(2):
                power = e[h, j, s]
                grad = dot(vbuf[pl.ds(base, BLOCK), cols], dot_[h, s])
                score = (power.astype(f32) * (grad - cen[h, s])).astype(bf16)
                dv_now = dot(power, don[h, s])
                dk_now = dot(score, qn[h, s])
                dv_part = dv_now if s == 0 else dv_part + dv_now
                dk_part = dk_now if s == 0 else dk_part + dk_now
                dq[h, s] += dot(kt[h, :, pl.ds(base, BLOCK)], score)
            dvs[pl.ds(base, BLOCK), cols] = dv_part.astype(bf16)
            dks[pl.ds(base, BLOCK), cols] = dk_part.astype(bf16)

        @pl.loop(0, 8)
        def _(n):
            @pl.when(jnp.logical_or(j > 0, n != me))
            def _():
                grad_copy(j, n, dvs, rv, dv_send, dv_recv).start()
                grad_copy(j, n, dks, rk, dk_send, dk_recv).start()

    self_copy(dvs, rv, dv_recv).start()
    self_copy(dks, rk, dk_recv).start()

    for s in range(2):
        for h in range(HEADS):
            for g in range(GROUP):
                rows = slice(g * ROWS, (g + 1) * ROWS)
                dqst[s, :, pl.ds((h * GROUP + g) * HD, HD)] = (
                    dq[h, s, :, rows].T * (weight * FACTOR)
                ).astype(bf16)
    dq_copies = put(dqst, dq_out, my_q, 3)
    for copy in dq_copies:
        copy.start()

    wide = jnp.concatenate([weight, weight], axis=1)
    pltpu.make_async_copy(rv, rv, dv_recv).wait()
    for n in range(4):
        total_v = rv[n * 8].astype(f32)
        for m in range(1, 8):
            total_v += rv[n * 8 + m].astype(f32)
        pvg_out[0, :, n * KCOLS : (n + 1) * KCOLS] = (total_v * wide).astype(bf16)
    pltpu.make_async_copy(rk, rk, dk_recv).wait()
    for n in range(4):
        total_k = rk[n * 8].astype(f32)
        for m in range(1, 8):
            total_k += rk[n * 8 + m].astype(f32)
        pkg_out[0, :, n * KCOLS : (n + 1) * KCOLS] = (total_k * (wide * FACTOR)).astype(bf16)

    push_done(pk, kbuf, k_send, k_recv)
    push_done(pv, vbuf, v_send, v_recv)
    for copy in pair:
        copy.wait_send()
    for step in range(1, 4):
        x_copy(step).wait_send()
        z_copy(step).wait_send()
        rest_copy(step).wait_send()

    @pl.loop(0, 32)
    def _(n):
        @pl.when(n != me)
        def _():
            grad_copy(n // 8, lax.rem(n, 8), dvs, rv, dv_send, dv_recv).wait_send()
            grad_copy(n // 8, lax.rem(n, 8), dks, rk, dk_send, dk_recv).wait_send()

    for local, remote in (o_copies, dk_copies, dv_copies, dq_copies):
        local.wait()
        remote.wait_send()
        remote.wait_recv()


def body(queries, keys, values, prefix_keys, prefix_values, lengths, out_grad):
    vmem = lambda shape, dtype: pltpu.VMEM(shape, dtype)
    dma = pltpu.SemaphoreType.DMA
    prefix = NBLOCK * BLOCK
    anywhere = pl.BlockSpec(memory_space=pl.ANY)
    in_vmem = pl.BlockSpec(memory_space=pltpu.VMEM)
    shape = lambda a: jax.ShapeDtypeStruct(a.shape, bf16)
    return pl.pallas_call(
        kernel,
        out_shape=[
            shape(queries), shape(queries), shape(keys), shape(values),
            shape(prefix_keys), shape(prefix_values),
        ],
        in_specs=[anywhere] * 5 + [pl.BlockSpec(memory_space=pltpu.SMEM), anywhere],
        out_specs=[anywhere] * 4 + [in_vmem] * 2,
        scratch_shapes=[
            vmem((LOCAL, 8 * HD), bf16), vmem((LOCAL, 8 * HD), bf16),
            vmem((2, ROWS, QCOLS), bf16), vmem((2, ROWS, QCOLS), bf16),
            vmem((2, ROWS, KCOLS), bf16), vmem((2, ROWS, KCOLS), bf16),
            vmem((prefix, KCOLS), bf16), vmem((prefix, KCOLS), bf16),
            vmem((3, 4, 8, 128), f32), vmem((2, 8, 128), f32),
            vmem((HEADS, 2, HD, CHUNK), bf16), vmem((HEADS, 2, CHUNK, HD), bf16),
            vmem((HEADS, 2, HD, CHUNK), bf16), vmem((HEADS, 2, CHUNK, HD), bf16),
            vmem((HEADS, HD + 16, prefix), bf16), vmem((HEADS, HD, prefix), bf16),
            vmem((HEADS, 2, HD, ROWS), bf16), vmem((HEADS, 2, HD + 16, ROWS), bf16),
            vmem((HEADS, NBLOCK, 2, BLOCK, CHUNK), bf16),
            vmem((HEADS, 2, ROWS, CHUNK), bf16),
            vmem((HEADS, 2, 8, CHUNK), f32),
            vmem((HEADS, 2, HD + 16, CHUNK), f32),
            vmem((HEADS, 2, 1, CHUNK), f32),
            vmem((HEADS, 2, HD, CHUNK), f32),
            vmem((2, ROWS, QCOLS), bf16), vmem((2, ROWS, QCOLS), bf16),
            vmem((2, ROWS, KCOLS), bf16), vmem((2, ROWS, KCOLS), bf16),
            vmem((prefix, KCOLS), bf16), vmem((prefix, KCOLS), bf16),
            vmem((32, LOCAL, KCOLS), bf16), vmem((32, LOCAL, KCOLS), bf16),
            dma((6,)), dma((5,)), dma((5,)), dma((1,)),
            dma((32,)), dma((32,)), dma((NBLOCK,)), dma((NBLOCK,)),
            dma((3, 3)), dma((3, 3)),
            dma((32,)), dma((32,)), dma, dma,
            dma((4,)), dma((4,)), dma((4,)),
        ],
        compiler_params=pltpu.CompilerParams(
            collective_id=0, has_side_effects=True, vmem_limit_bytes=60 * 2**20
        ),
        cost_estimate=pl.CostEstimate(
            flops=14 * 2**30, bytes_accessed=10 * 2**20, transcendentals=9 * 2**20
        ),
    )(queries, keys, values, prefix_keys, prefix_values, lengths, out_grad)


def solution(mesh):
    in_specs = (
        P("prompt", "response", "tensor"),
        P("prompt", "response", "tensor"),
        P("prompt", "response", "tensor"),
        P("prompt", ("response", "tensor"), None),
        P("prompt", ("response", "tensor"), None),
        P("prompt", "response"),
        P("prompt", "response", "tensor"),
    )
    out_specs = (
        P("prompt", "response", "tensor"),
        P("prompt", "response", "tensor"),
        P("prompt", "response", "tensor"),
        P("prompt", "response", "tensor"),
        P("prompt", ("response", "tensor"), None),
        P("prompt", ("response", "tensor"), None),
    )
    return jax.shard_map(body, mesh=mesh, in_specs=in_specs, out_specs=out_specs, check_vma=False)
```

```python
import math

import jax
import jax.numpy as jnp
from jax import lax
from jax.experimental import pallas as pl
from jax.experimental.pallas import tpu as pltpu
from jax.sharding import PartitionSpec as P

HD = 128
GROUP = 8
ROWS = 128
LOCAL = 64
BLOCK = 512
NBLOCK = 4
CHUNK = 1024
HALF = 512
HEADS = 2
QCOLS = HEADS * GROUP * HD
KCOLS = HEADS * HD
FACTOR = 1.0 / math.sqrt(HD)
EXP2 = math.log2(math.e) * FACTOR
MESH = pl.DeviceIdType.MESH
f32 = jnp.float32
bf16 = jnp.bfloat16


def dot(a, b):
    return jnp.dot(a, b, preferred_element_type=f32)


def kernel(
    q_in, k_in, v_in, pk_in, pv_in, len_in, do_in,
    o_out, dq_out, dk_out, dv_out, pkg_out, pvg_out,
    pk, pv, qin, din, kown, vown, kbuf, vbuf, lens, lsum,
    qt, qn, dot_, don, vt, kt, kot, vot, e, eo, mx, acc, cen, dq,
    ost, dqst, dkst, dvst, dkv, rkv, far,
    load_sem, pair_send, pair_recv, k_send, v_send, k_recv, v_recv,
    len_send, len_recv, grad_send, grad_recv, far_recv, out_send, out_recv, out_sem,
):
    prompt = lax.axis_index("prompt")
    resp = lax.axis_index("response")
    y_hi = lax.axis_index("tensor")
    core = lax.rem(resp, 2)
    z = lax.rem(resp // 2, 4)
    y_lo = resp // 8
    y = y_hi * 2 + y_lo
    other = 1 - core

    def at(zz, yy, cc):
        return {"response": lax.rem(yy, 2) * 8 + zz * 2 + cc, "tensor": yy // 2}

    def along_x(pp):
        return {"prompt": pp}

    sibling = {"response": resp + 1 - 2 * core}
    my_q = pl.ds(pl.multiple_of(core * QCOLS, QCOLS), QCOLS)
    its_q = pl.ds(pl.multiple_of(other * QCOLS, QCOLS), QCOLS)
    my_k = pl.ds(pl.multiple_of(core * KCOLS, KCOLS), KCOLS)
    its_k = pl.ds(pl.multiple_of(other * KCOLS, KCOLS), KCOLS)

    loads = [
        pltpu.make_async_copy(pk_in.at[0], pk, load_sem.at[0]),
        pltpu.make_async_copy(pv_in.at[0], pv, load_sem.at[1]),
        pltpu.make_async_copy(q_in.at[0, :, my_q], qin.at[0], load_sem.at[2]),
        pltpu.make_async_copy(do_in.at[0, :, my_q], din.at[0], load_sem.at[3]),
        pltpu.make_async_copy(k_in.at[0, :, my_k], kown.at[0], load_sem.at[4]),
        pltpu.make_async_copy(v_in.at[0, :, my_k], vown.at[0], load_sem.at[5]),
    ]
    for copy in loads:
        copy.start()

    barrier = pltpu.get_barrier_semaphore()

    def greet(device):
        pl.semaphore_signal(barrier, inc=1, device_id=device, device_id_type=MESH)

    for dist in (1, 3, 0):
        for n in range(8):
            if dist or n:
                greet(
                    at(
                        lax.rem(z + dist, 4),
                        lax.rem(y + n // 2, 4),
                        lax.rem(core + n % 2, 2),
                    )
                )
    greet(at(lax.rem(z + 2, 4), y, core))
    for step in range(1, 4):
        greet(along_x(lax.rem(prompt + step, 4)))
    pl.semaphore_wait(barrier, 27)

    def send(src, dst, send_sem, recv_sem, device):
        return pltpu.make_async_remote_copy(
            src_ref=src,
            dst_ref=dst,
            send_sem=send_sem,
            recv_sem=recv_sem,
            device_id=device,
            device_id_type=MESH,
        )

    lens[0, prompt] = jnp.full((8, 128), len_in[0, 0], jnp.int32).astype(f32)
    pair = [
        send(lens.at[0, prompt], lsum.at[1], pair_send.at[0], pair_recv.at[0], sibling),
        send(q_in.at[0, :, its_q], qin.at[1], pair_send.at[1], pair_recv.at[1], sibling),
        send(k_in.at[0, :, its_k], kown.at[1], pair_send.at[2], pair_recv.at[2], sibling),
        send(do_in.at[0, :, its_q], din.at[1], pair_send.at[3], pair_recv.at[3], sibling),
        send(v_in.at[0, :, its_k], vown.at[1], pair_send.at[4], pair_recv.at[4], sibling),
    ]
    lsum[0] = lens[0, prompt]
    pair[0].start()
    pair[1].start()
    pair[2].start()

    my_row = pl.multiple_of((y * 2 + core) * LOCAL, LOCAL)
    up, down = lax.rem(z + 1, 4), lax.rem(z + 3, 4)
    routes = ((0, lax.rem(z + 3 + 2 * y_hi, 4)), (1, z), (2, lax.rem(z + 5 - 2 * y_hi, 4)))

    def push(shard, buf, send_sems, recv_sems):
        for block, to_z in routes:
            for n in range(8):
                if block == 1 and n == 0:
                    continue
                to_y = lax.rem(y + n // 2, 4)
                to_core = lax.rem(core + n % 2, 2)
                cols = pl.multiple_of(((to_y // 2) * 2 + to_core) * KCOLS, KCOLS)
                send(
                    shard.at[:, pl.ds(cols, KCOLS)],
                    buf.at[pl.ds(block * BLOCK + my_row, LOCAL)],
                    send_sems.at[0],
                    recv_sems.at[block],
                    at(to_z, to_y, to_core),
                ).start()

    def passing(buf, send_sems, recv_sems):
        half = BLOCK // 2
        return [
            send(
                buf.at[pl.ds(n * half, half)],
                buf.at[pl.ds(3 * BLOCK + n * half, half)],
                send_sems.at[1 + n],
                recv_sems.at[3],
                at(down if n == 0 else up, y, core),
            )
            for n in range(2)
        ]

    def push_done(buf, send_sems, recv_sems):
        sent = buf.at[pl.ds(0, 23 * LOCAL)]
        pltpu.make_async_copy(sent, sent, send_sems.at[0]).wait()
        for copy in passing(buf, send_sems, recv_sems):
            copy.wait_send()

    mine = pl.ds(pl.multiple_of((y_hi * 2 + core) * KCOLS, KCOLS), KCOLS)
    loads[0].wait()
    push(pk, kbuf, k_send, k_recv)
    pltpu.make_async_copy(pk.at[:, mine], kbuf.at[pl.ds(BLOCK + my_row, LOCAL)], k_recv.at[1]).start()
    pair[3].start()
    pair[4].start()
    loads[1].wait()
    pltpu.make_async_copy(pv.at[:, mine], vbuf.at[pl.ds(BLOCK + my_row, LOCAL)], v_recv.at[1]).start()

    def x_copy(step):
        return send(
            lens.at[0, prompt], lens.at[0, prompt], len_send.at[0, step - 1],
            len_recv.at[0, step - 1], along_x(lax.rem(prompt + step, 4)),
        )

    def z_copy(step):
        return send(
            lens.at[1, z], lens.at[1, z], len_send.at[1, step - 1],
            len_recv.at[1, step - 1], at(lax.rem(z + step, 4), y, core),
        )

    rest = y_lo * 2 + core

    def rest_copy(step):
        slot = lax.rem(rest + step, 4)
        return send(
            lens.at[2, rest], lens.at[2, rest], len_send.at[2, step - 1],
            len_recv.at[2, step - 1], at(z, y_hi * 2 + slot // 2, lax.rem(slot, 2)),
        )

    for step in range(1, 4):
        x_copy(step).start()

    slot_row = lax.broadcasted_iota(jnp.int32, (ROWS, HD), 0).astype(f32)

    def stage_q(s):
        for h in range(HEADS):
            for g in range(GROUP):
                cols = pl.ds((h * GROUP + g) * HD, HD)
                block = qin[s, :, cols]
                qn[h, s, g * ROWS : (g + 1) * ROWS, :] = block
                qt[h, s, :, g * ROWS : (g + 1) * ROWS] = block.T

    def stage_do(s):
        live = slot_row < lsum[s, 0:1, :]
        for h in range(HEADS):
            for g in range(GROUP):
                cols = pl.ds((h * GROUP + g) * HD, HD)
                block = jnp.where(live, din[s, :, cols].astype(f32), 0.0).astype(bf16)
                dot_[h, s, :, g * ROWS : (g + 1) * ROWS] = block.T

    def stage_own(s):
        for h in range(HEADS):
            cols = pl.ds(h * HD, HD)
            kot[h, s] = kown[s, :, cols].T
            vot[h, s, 0:HD] = vown[s, :, cols].T
            vot[h, s, HD : HD + 16] = jnp.ones((16, ROWS), bf16)

    allowed = lax.broadcasted_iota(jnp.int32, (ROWS, HALF), 0) <= lax.rem(
        lax.broadcasted_iota(jnp.int32, (ROWS, HALF), 1), ROWS
    )

    def own_scores(h, s, part):
        scores = dot(kown[s, :, pl.ds(h * HD, HD)], qt[h, s, :, part * HALF : (part + 1) * HALF])
        return jnp.where(allowed, scores, -1e30)

    def own_max(s):
        for h in range(HEADS):
            for part in range(2):
                cols = pl.ds(part * HALF, HALF)
                mx[h, s, :, cols] = jnp.max(
                    own_scores(h, s, part).reshape(ROWS // 8, 8, HALF), axis=0
                )

    loads[2].wait()
    loads[4].wait()
    stage_q(0)
    own_max(0)
    loads[3].wait()
    stage_do(0)
    loads[5].wait()
    stage_own(0)
    for h in range(HEADS):
        vt[h, HD : HD + 16] = jnp.ones((16, NBLOCK * BLOCK), bf16)
    pair[0].wait_recv()
    pair[1].wait_recv()
    pair[2].wait_recv()
    stage_q(1)
    own_max(1)

    @pl.loop(0, NBLOCK)
    def _(j):
        base = pl.multiple_of(j * BLOCK, BLOCK)
        keys = kbuf.at[pl.ds(base, BLOCK)]
        pltpu.make_async_copy(keys, keys, k_recv.at[j]).wait()

        @pl.when(j == 0)
        def _():
            for copy in passing(kbuf, k_send, k_recv):
                copy.start()
            push(pv, vbuf, v_send, v_recv)

        for h in range(HEADS):
            cols = pl.ds(h * HD, HD)
            for n in range(BLOCK // 128):
                kt[h, :, pl.ds(base + n * 128, 128)] = kbuf[pl.ds(base + n * 128, 128), cols].T
            for s in range(2):
                for part in range(2):
                    rows = pl.ds(part * HALF, HALF)
                    scores = dot(kbuf[pl.ds(base, BLOCK), cols], qt[h, s, :, rows])
                    mx[h, s, :, rows] = jnp.maximum(
                        mx[h, s, :, rows],
                        jnp.max(scores.reshape(BLOCK // 8, 8, HALF), axis=0),
                    )

    for step in range(1, 4):
        x_copy(step).wait_recv()
    lens[1, z] = lens[0, 0] + lens[0, 1] + lens[0, 2] + lens[0, 3]
    for step in range(1, 4):
        z_copy(step).start()

    pair[3].wait_recv()
    pair[4].wait_recv()
    stage_do(1)
    stage_own(1)

    for h in range(HEADS):
        for s in range(2):
            top = jnp.max(mx[h, s], axis=0, keepdims=True) * EXP2
            mx[h, s] = jnp.broadcast_to(top, (8, CHUNK))
            for part in range(2):
                rows = pl.ds(part * HALF, HALF)
                power = jnp.exp2(own_scores(h, s, part) * EXP2 - mx[h, s, 0:1, rows]).astype(bf16)
                eo[h, s, :, rows] = power
                acc[h, s, :, rows] = dot(vot[h, s], power)

    @pl.loop(0, NBLOCK)
    def _(j):
        base = pl.multiple_of(j * BLOCK, BLOCK)
        vals = vbuf.at[pl.ds(base, BLOCK)]
        pltpu.make_async_copy(vals, vals, v_recv.at[j]).wait()

        @pl.when(j == 0)
        def _():
            for copy in passing(vbuf, v_send, v_recv):
                copy.start()

        for h in range(HEADS):
            cols = pl.ds(h * HD, HD)
            for n in range(BLOCK // 128):
                vt[h, 0:HD, pl.ds(base + n * 128, 128)] = vbuf[
                    pl.ds(base + n * 128, 128), cols
                ].T
            for s in range(2):
                for part in range(2):
                    rows = pl.ds(part * HALF, HALF)
                    scores = dot(kbuf[pl.ds(base, BLOCK), cols], qt[h, s, :, rows])
                    power = jnp.exp2(scores * EXP2 - mx[h, s, 0:1, rows]).astype(bf16)
                    e[h, j, s, :, rows] = power
                    acc[h, s, :, rows] += dot(vt[h, :, pl.ds(base, BLOCK)], power)

    for step in range(1, 4):
        z_copy(step).wait_recv()
    lens[2, rest] = lens[1, 0] + lens[1, 1] + lens[1, 2] + lens[1, 3]
    for step in range(1, 4):
        rest_copy(step).start()

    def put(src, out, dst_cols, n):
        return (
            pltpu.make_async_copy(src.at[0], out.at[0, :, dst_cols], out_sem.at[n]),
            send(src.at[1], out.at[0, :, dst_cols], out_send.at[n], out_recv.at[n], sibling),
        )

    for s in range(2):
        for h in range(HEADS):
            inv = 1.0 / acc[h, s, HD : HD + 1, :]
            acc[h, s, HD : HD + 1, :] = inv
            cotangent = dot_[h, s].astype(f32)
            total = jnp.sum(acc[h, s, 0:HD, :] * cotangent, axis=0, keepdims=True)
            cen[h, s] = total * inv * inv
            scaled = (cotangent * inv).astype(bf16)
            dot_[h, s] = scaled
            for g in range(GROUP):
                rows = slice(g * ROWS, (g + 1) * ROWS)
                don[h, s, rows, :] = scaled[:, rows].T

    half_rows = BLOCK // 2

    def grad_copy(j, half, n):
        dist = (1 - j) * (1 - 2 * half)
        slot = (y_hi * 2 + core) * 6 + lax.rem(dist + 3, 3) * 2 + y_lo
        row = pl.multiple_of(j * BLOCK + half * half_rows + n * LOCAL, LOCAL)
        return send(
            dkv.at[pl.ds(row, LOCAL)],
            rkv.at[slot],
            grad_send.at[0],
            grad_recv,
            at(lax.rem(z + dist + 4, 4), half * 2 + n // 2, n % 2),
        )

    def far_copy(half):
        row = pl.multiple_of(3 * BLOCK + half * half_rows, half_rows)
        return send(
            dkv.at[pl.ds(row, half_rows)],
            far.at[half],
            grad_send.at[1 + half],
            far_recv.at[half],
            at(lax.rem(z + 1 + 2 * half, 4), y, core),
        )

    me = y * 2 + core

    for h in range(HEADS):
        for s in range(2):
            dq[h, s] = jnp.zeros((HD, CHUNK), f32)

    @pl.loop(0, 2 * NBLOCK)
    def _(step):
        turn = step // 2
        j = (1 - turn // 2) * (3 - turn) + (turn // 2) * (turn - 2)
        half = lax.rem(step + turn * (2 - turn) * (3 - turn) // 2, 2)
        base = pl.multiple_of(j * BLOCK + half * half_rows, half_rows)
        inner = pl.ds(pl.multiple_of(half * half_rows, half_rows), half_rows)
        rows = pl.ds(base, half_rows)
        for h in range(HEADS):
            cols = pl.ds(h * HD, HD)
            dv_part = None
            dk_part = None
            for s in range(2):
                power = e[h, j, s, inner]
                grad = dot(vbuf[rows, cols], dot_[h, s])
                score = (power.astype(f32) * (grad - cen[h, s])).astype(bf16)
                dv_now = dot(power, don[h, s])
                dk_now = dot(score, qn[h, s])
                dv_part = dv_now if s == 0 else dv_part + dv_now
                dk_part = dk_now if s == 0 else dk_part + dk_now
                dq[h, s] += dot(kt[h, :, pl.ds(base, half_rows)], score)
            dkv[rows, pl.ds(h * HD, HD)] = dk_part.astype(bf16)
            dkv[rows, pl.ds(KCOLS + h * HD, HD)] = dv_part.astype(bf16)

        @pl.when(turn == 0)
        def _():
            far_copy(half).start()

        @pl.when(turn == 2)
        def _():
            pltpu.make_async_copy(far.at[half], far.at[half], far_recv.at[half]).wait()
            dkv[rows] = (dkv[rows].astype(f32) + far[half].astype(f32)).astype(bf16)

        @pl.when(turn > 0)
        def _():
            for n in range(4):

                @pl.when(jnp.logical_or(j != 1, half * 4 + n != me))
                def _():
                    grad_copy(j, half, n).start()

    pltpu.make_async_copy(
        dkv.at[pl.ds(BLOCK + my_row, LOCAL)], rkv.at[(y_hi * 2 + core) * 6 + y_lo], grad_recv
    ).start()

    for s in range(2):
        live = slot_row < lsum[s, 0:1, :]
        for h in range(HEADS):
            attended = acc[h, s, 0:HD, :] * acc[h, s, HD : HD + 1, :]
            for g in range(GROUP):
                rows = slice(g * ROWS, (g + 1) * ROWS)
                ost[s, :, pl.ds((h * GROUP + g) * HD, HD)] = jnp.where(
                    live, attended[:, rows].T, 0.0
                ).astype(bf16)
    o_copies = put(ost, o_out, my_q, 0)
    o_copies[0].start()
    o_copies[1].start()

    for step in range(1, 4):
        rest_copy(step).wait_recv()
    total = lens[2, 0] + lens[2, 1] + lens[2, 2] + lens[2, 3]
    weight = (4.0 * 16.0 * ROWS) / total[0:1, :]

    for h in range(HEADS):
        cols = pl.ds(h * HD, HD)
        for s in range(2):
            power = eo[h, s]
            grad = dot(vown[s, :, cols], dot_[h, s])
            score = (power.astype(f32) * (grad - cen[h, s])).astype(bf16)
            dvst[s, :, cols] = (dot(power, don[h, s]) * weight).astype(bf16)
            dkst[s, :, cols] = (dot(score, qn[h, s]) * (weight * FACTOR)).astype(bf16)
            dq[h, s] += dot(kot[h, s], score)
    dk_copies = put(dkst, dk_out, my_k, 1)
    dv_copies = put(dvst, dv_out, my_k, 2)
    for copy in dk_copies + dv_copies:
        copy.start()

    for s in range(2):
        for h in range(HEADS):
            for g in range(GROUP):
                rows = slice(g * ROWS, (g + 1) * ROWS)
                dqst[s, :, pl.ds((h * GROUP + g) * HD, HD)] = (
                    dq[h, s, :, rows].T * (weight * FACTOR)
                ).astype(bf16)
    dq_copies = put(dqst, dq_out, my_q, 3)
    for copy in dq_copies:
        copy.start()

    push_done(kbuf, k_send, k_recv)
    push_done(vbuf, v_send, v_recv)
    for copy in pair:
        copy.wait_send()
    for step in range(1, 4):
        x_copy(step).wait_send()
        z_copy(step).wait_send()
        rest_copy(step).wait_send()
    for half in range(2):
        far_copy(half).wait_send()
    for local, remote in (o_copies, dk_copies, dv_copies):
        local.wait()
        remote.wait_send()
        remote.wait_recv()
    sent = dkv.at[pl.ds(0, 23 * LOCAL)]
    pltpu.make_async_copy(sent, sent, grad_send.at[0]).wait()

    pltpu.make_async_copy(rkv, rkv, grad_recv).wait()
    twice = jnp.concatenate([weight, weight], axis=1)
    for n in range(4):
        summed = rkv[n * 6].astype(f32)
        for m in range(1, 6):
            summed += rkv[n * 6 + m].astype(f32)
        cols = slice(n * KCOLS, (n + 1) * KCOLS)
        pkg_out[0, :, cols] = (summed[:, :KCOLS] * (twice * FACTOR)).astype(bf16)
        pvg_out[0, :, cols] = (summed[:, KCOLS:] * twice).astype(bf16)
    dq_copies[0].wait()
    dq_copies[1].wait_send()
    dq_copies[1].wait_recv()


def copy_kernel(*refs):
    sources, results, held, (come, go) = refs[:6], refs[6:12], refs[12:18], refs[18:]
    loads = [pltpu.make_async_copy(sources[n], held[n], come.at[n]) for n in range(6)]
    stores = [pltpu.make_async_copy(held[n], results[n], go.at[n]) for n in range(6)]
    for copy in loads:
        copy.start()
    for n in range(6):
        loads[n].wait()
        stores[n].start()
    for copy in stores:
        copy.wait()


def body(queries, keys, values, prefix_keys, prefix_values, lengths, out_grad):
    vmem = lambda shape, dtype: pltpu.VMEM(shape, dtype)
    dma = pltpu.SemaphoreType.DMA
    prefix = NBLOCK * BLOCK
    anywhere = pl.BlockSpec(memory_space=pl.ANY)
    in_vmem = pl.BlockSpec(memory_space=pltpu.VMEM)
    shape = lambda a: jax.ShapeDtypeStruct(a.shape, bf16)
    results = pl.pallas_call(
        kernel,
        out_shape=[
            shape(queries), shape(queries), shape(keys), shape(values),
            shape(prefix_keys), shape(prefix_values),
        ],
        in_specs=[anywhere] * 5 + [pl.BlockSpec(memory_space=pltpu.SMEM), anywhere],
        out_specs=[anywhere] * 4 + [in_vmem] * 2,
        scratch_shapes=[
            vmem((LOCAL, 8 * HD), bf16), vmem((LOCAL, 8 * HD), bf16),
            vmem((2, ROWS, QCOLS), bf16), vmem((2, ROWS, QCOLS), bf16),
            vmem((2, ROWS, KCOLS), bf16), vmem((2, ROWS, KCOLS), bf16),
            vmem((prefix, KCOLS), bf16), vmem((prefix, KCOLS), bf16),
            vmem((3, 4, 8, 128), f32), vmem((2, 8, 128), f32),
            vmem((HEADS, 2, HD, CHUNK), bf16), vmem((HEADS, 2, CHUNK, HD), bf16),
            vmem((HEADS, 2, HD, CHUNK), bf16), vmem((HEADS, 2, CHUNK, HD), bf16),
            vmem((HEADS, HD + 16, prefix), bf16), vmem((HEADS, HD, prefix), bf16),
            vmem((HEADS, 2, HD, ROWS), bf16), vmem((HEADS, 2, HD + 16, ROWS), bf16),
            vmem((HEADS, NBLOCK, 2, BLOCK, CHUNK), bf16),
            vmem((HEADS, 2, ROWS, CHUNK), bf16),
            vmem((HEADS, 2, 8, CHUNK), f32),
            vmem((HEADS, 2, HD + 16, CHUNK), f32),
            vmem((HEADS, 2, 1, CHUNK), f32),
            vmem((HEADS, 2, HD, CHUNK), f32),
            vmem((2, ROWS, QCOLS), bf16), vmem((2, ROWS, QCOLS), bf16),
            vmem((2, ROWS, KCOLS), bf16), vmem((2, ROWS, KCOLS), bf16),
            vmem((prefix, 2 * KCOLS), bf16),
            vmem((24, LOCAL, 2 * KCOLS), bf16),
            vmem((2, BLOCK // 2, 2 * KCOLS), bf16),
            dma((6,)), dma((5,)), dma((5,)),
            dma((3,)), dma((3,)), dma((NBLOCK,)), dma((NBLOCK,)),
            dma((3, 3)), dma((3, 3)),
            dma((3,)), dma, dma((2,)),
            dma((4,)), dma((4,)), dma((4,)),
        ],
        compiler_params=pltpu.CompilerParams(
            collective_id=0, has_side_effects=True, vmem_limit_bytes=60 * 2**20
        ),
        cost_estimate=pl.CostEstimate(
            flops=14 * 2**30, bytes_accessed=10 * 2**20, transcendentals=9 * 2**20
        ),
    )(queries, keys, values, prefix_keys, prefix_values, lengths, out_grad)
    return pl.pallas_call(
        copy_kernel,
        out_shape=[jax.ShapeDtypeStruct(a.shape, a.dtype) for a in results],
        in_specs=[anywhere] * 6,
        out_specs=[anywhere] * 6,
        scratch_shapes=[vmem(a.shape, a.dtype) for a in results] + [dma((6,)), dma((6,))],
    )(*results)


def solution(mesh):
    in_specs = (
        P("prompt", "response", "tensor"),
        P("prompt", "response", "tensor"),
        P("prompt", "response", "tensor"),
        P("prompt", ("response", "tensor"), None),
        P("prompt", ("response", "tensor"), None),
        P("prompt", "response"),
        P("prompt", "response", "tensor"),
    )
    out_specs = (
        P("prompt", "response", "tensor"),
        P("prompt", "response", "tensor"),
        P("prompt", "response", "tensor"),
        P("prompt", "response", "tensor"),
        P("prompt", ("response", "tensor"), None),
        P("prompt", ("response", "tensor"), None),
    )
    return jax.shard_map(body, mesh=mesh, in_specs=in_specs, out_specs=out_specs, check_vma=False)
```

```python
import math

import jax
import jax.numpy as jnp
from jax import lax
from jax.experimental import pallas as pl
from jax.experimental.pallas import tpu as pltpu
from jax.sharding import PartitionSpec as P

HD = 128
GROUP = 8
ROWS = 128
LOCAL = 64
BLOCK = 512
NBLOCK = 4
CHUNK = 1024
HALF = 512
HEADS = 2
QCOLS = HEADS * GROUP * HD
KCOLS = HEADS * HD
FACTOR = 1.0 / math.sqrt(HD)
EXP2 = math.log2(math.e) * FACTOR
MESH = pl.DeviceIdType.MESH
f32 = jnp.float32
bf16 = jnp.bfloat16


def dot(a, b):
    return jnp.dot(a, b, preferred_element_type=f32)


def kernel(
    q_in, k_in, v_in, pk_in, pv_in, len_in, do_in,
    o_out, dq_out, dk_out, dv_out, pkg_out, pvg_out,
    pk, pv, qin, din, kown, vown, kbuf, vbuf, lens, lsum,
    qt, qn, dot_, don, vt, kt, kot, vot, e, eo, mx, acc, cen, dq,
    ost, dqst, dkst, dvst, dkv, rkv, far,
    load_sem, pair_send, pair_recv, k_send, v_send, k_recv, v_recv,
    len_send, len_recv, grad_send, grad_recv, far_recv, out_send, out_recv, out_sem,
):
    prompt = lax.axis_index("prompt")
    resp = lax.axis_index("response")
    y_hi = lax.axis_index("tensor")
    core = lax.rem(resp, 2)
    z = lax.rem(resp // 2, 4)
    y_lo = resp // 8
    y = y_hi * 2 + y_lo
    other = 1 - core

    def at(zz, yy, cc):
        return {"response": lax.rem(yy, 2) * 8 + zz * 2 + cc, "tensor": yy // 2}

    def along_x(pp):
        return {"prompt": pp}

    sibling = {"response": resp + 1 - 2 * core}
    my_q = pl.ds(pl.multiple_of(core * QCOLS, QCOLS), QCOLS)
    its_q = pl.ds(pl.multiple_of(other * QCOLS, QCOLS), QCOLS)
    my_k = pl.ds(pl.multiple_of(core * KCOLS, KCOLS), KCOLS)
    its_k = pl.ds(pl.multiple_of(other * KCOLS, KCOLS), KCOLS)

    loads = [
        pltpu.make_async_copy(pk_in.at[0], pk, load_sem.at[0]),
        pltpu.make_async_copy(pv_in.at[0], pv, load_sem.at[1]),
        pltpu.make_async_copy(q_in.at[0, :, my_q], qin.at[0], load_sem.at[2]),
        pltpu.make_async_copy(do_in.at[0, :, my_q], din.at[0], load_sem.at[3]),
        pltpu.make_async_copy(k_in.at[0, :, my_k], kown.at[0], load_sem.at[4]),
        pltpu.make_async_copy(v_in.at[0, :, my_k], vown.at[0], load_sem.at[5]),
    ]
    for copy in loads:
        copy.start()

    barrier = pltpu.get_barrier_semaphore()

    def greet(device):
        pl.semaphore_signal(barrier, inc=1, device_id=device, device_id_type=MESH)

    for dist in (1, 3, 0):
        for n in range(8):
            if dist or n:
                greet(
                    at(
                        lax.rem(z + dist, 4),
                        lax.rem(y + n // 2, 4),
                        lax.rem(core + n % 2, 2),
                    )
                )
    greet(at(lax.rem(z + 2, 4), y, core))
    for step in range(1, 4):
        greet(along_x(lax.rem(prompt + step, 4)))
    pl.semaphore_wait(barrier, 27)

    def send(src, dst, send_sem, recv_sem, device):
        return pltpu.make_async_remote_copy(
            src_ref=src,
            dst_ref=dst,
            send_sem=send_sem,
            recv_sem=recv_sem,
            device_id=device,
            device_id_type=MESH,
        )

    lens[0, prompt] = jnp.full((8, 128), len_in[0, 0], jnp.int32).astype(f32)
    pair = [
        send(lens.at[0, prompt], lsum.at[1], pair_send.at[0], pair_recv.at[0], sibling),
        send(q_in.at[0, :, its_q], qin.at[1], pair_send.at[1], pair_recv.at[1], sibling),
        send(k_in.at[0, :, its_k], kown.at[1], pair_send.at[2], pair_recv.at[2], sibling),
        send(do_in.at[0, :, its_q], din.at[1], pair_send.at[3], pair_recv.at[3], sibling),
        send(v_in.at[0, :, its_k], vown.at[1], pair_send.at[4], pair_recv.at[4], sibling),
    ]
    lsum[0] = lens[0, prompt]
    pair[0].start()
    pair[1].start()
    pair[2].start()

    my_row = pl.multiple_of((core * 4 + y) * LOCAL, LOCAL)
    up, down = lax.rem(z + 1, 4), lax.rem(z + 3, 4)
    routes = ((0, lax.rem(z + 3 + 2 * core, 4)), (1, z), (2, lax.rem(z + 5 - 2 * core, 4)))

    def push(shard, buf, send_sems, recv_sems):
        for block, to_z in routes:
            for n in range(8):
                if block == 1 and n == 0:
                    continue
                to_y = lax.rem(y + n // 2, 4)
                to_core = lax.rem(core + n % 2, 2)
                cols = pl.multiple_of(((to_y // 2) * 2 + to_core) * KCOLS, KCOLS)
                send(
                    shard.at[:, pl.ds(cols, KCOLS)],
                    buf.at[pl.ds(block * BLOCK + my_row, LOCAL)],
                    send_sems.at[0],
                    recv_sems.at[block],
                    at(to_z, to_y, to_core),
                ).start()

    def passing(buf, send_sems, recv_sems):
        half = BLOCK // 2
        return [
            send(
                buf.at[pl.ds(n * half, half)],
                buf.at[pl.ds(3 * BLOCK + n * half, half)],
                send_sems.at[1 + n],
                recv_sems.at[3],
                at(down if n == 0 else up, y, core),
            )
            for n in range(2)
        ]

    def push_done(buf, send_sems, recv_sems):
        sent = buf.at[pl.ds(0, 23 * LOCAL)]
        pltpu.make_async_copy(sent, sent, send_sems.at[0]).wait()
        for copy in passing(buf, send_sems, recv_sems):
            copy.wait_send()

    mine = pl.ds(pl.multiple_of((y_hi * 2 + core) * KCOLS, KCOLS), KCOLS)
    loads[0].wait()
    push(pk, kbuf, k_send, k_recv)
    pltpu.make_async_copy(pk.at[:, mine], kbuf.at[pl.ds(BLOCK + my_row, LOCAL)], k_recv.at[1]).start()
    pair[3].start()
    pair[4].start()
    loads[1].wait()
    pltpu.make_async_copy(pv.at[:, mine], vbuf.at[pl.ds(BLOCK + my_row, LOCAL)], v_recv.at[1]).start()

    def x_copy(step):
        return send(
            lens.at[0, prompt], lens.at[0, prompt], len_send.at[0, step - 1],
            len_recv.at[0, step - 1], along_x(lax.rem(prompt + step, 4)),
        )

    def z_copy(step):
        return send(
            lens.at[1, z], lens.at[1, z], len_send.at[1, step - 1],
            len_recv.at[1, step - 1], at(lax.rem(z + step, 4), y, core),
        )

    rest = y_lo * 2 + core

    def rest_copy(step):
        slot = lax.rem(rest + step, 4)
        return send(
            lens.at[2, rest], lens.at[2, rest], len_send.at[2, step - 1],
            len_recv.at[2, step - 1], at(z, y_hi * 2 + slot // 2, lax.rem(slot, 2)),
        )

    for step in range(1, 4):
        x_copy(step).start()

    slot_row = lax.broadcasted_iota(jnp.int32, (ROWS, HD), 0).astype(f32)

    def stage_q(s):
        for h in range(HEADS):
            for g in range(GROUP):
                cols = pl.ds((h * GROUP + g) * HD, HD)
                block = qin[s, :, cols]
                qn[h, s, g * ROWS : (g + 1) * ROWS, :] = block
                qt[h, s, :, g * ROWS : (g + 1) * ROWS] = block.T

    def stage_do(s):
        live = slot_row < lsum[s, 0:1, :]
        for h in range(HEADS):
            for g in range(GROUP):
                cols = pl.ds((h * GROUP + g) * HD, HD)
                block = jnp.where(live, din[s, :, cols].astype(f32), 0.0).astype(bf16)
                dot_[h, s, :, g * ROWS : (g + 1) * ROWS] = block.T

    def stage_own(s):
        for h in range(HEADS):
            cols = pl.ds(h * HD, HD)
            kot[h, s] = kown[s, :, cols].T
            vot[h, s, 0:HD] = vown[s, :, cols].T
            vot[h, s, HD : HD + 16] = jnp.ones((16, ROWS), bf16)

    allowed = lax.broadcasted_iota(jnp.int32, (ROWS, HALF), 0) <= lax.rem(
        lax.broadcasted_iota(jnp.int32, (ROWS, HALF), 1), ROWS
    )

    def own_scores(h, s, part):
        scores = dot(kown[s, :, pl.ds(h * HD, HD)], qt[h, s, :, part * HALF : (part + 1) * HALF])
        return jnp.where(allowed, scores, -1e30)

    def own_max(s):
        for h in range(HEADS):
            for part in range(2):
                cols = pl.ds(part * HALF, HALF)
                mx[h, s, :, cols] = jnp.max(
                    own_scores(h, s, part).reshape(ROWS // 8, 8, HALF), axis=0
                )

    loads[2].wait()
    loads[4].wait()
    stage_q(0)
    own_max(0)
    loads[3].wait()
    stage_do(0)
    loads[5].wait()
    stage_own(0)
    for h in range(HEADS):
        vt[h, HD : HD + 16] = jnp.ones((16, NBLOCK * BLOCK), bf16)
    pair[0].wait_recv()
    pair[1].wait_recv()
    pair[2].wait_recv()
    stage_q(1)
    own_max(1)

    push(pv, vbuf, v_send, v_recv)
    @pl.loop(0, NBLOCK)
    def _(j):
        base = pl.multiple_of(j * BLOCK, BLOCK)
        keys = kbuf.at[pl.ds(base, BLOCK)]
        pltpu.make_async_copy(keys, keys, k_recv.at[j]).wait()

        @pl.when(j == 0)
        def _():
            for copy in passing(kbuf, k_send, k_recv):
                copy.start()

        for h in range(HEADS):
            cols = pl.ds(h * HD, HD)
            for n in range(BLOCK // 128):
                kt[h, :, pl.ds(base + n * 128, 128)] = kbuf[pl.ds(base + n * 128, 128), cols].T
            for s in range(2):
                for part in range(2):
                    rows = pl.ds(part * HALF, HALF)
                    scores = dot(kbuf[pl.ds(base, BLOCK), cols], qt[h, s, :, rows])
                    mx[h, s, :, rows] = jnp.maximum(
                        mx[h, s, :, rows],
                        jnp.max(scores.reshape(BLOCK // 8, 8, HALF), axis=0),
                    )

    for step in range(1, 4):
        x_copy(step).wait_recv()
    lens[1, z] = lens[0, 0] + lens[0, 1] + lens[0, 2] + lens[0, 3]
    for step in range(1, 4):
        z_copy(step).start()

    pair[3].wait_recv()
    pair[4].wait_recv()
    stage_do(1)
    stage_own(1)

    for h in range(HEADS):
        for s in range(2):
            top = jnp.max(mx[h, s], axis=0, keepdims=True) * EXP2
            mx[h, s] = jnp.broadcast_to(top, (8, CHUNK))
            for part in range(2):
                rows = pl.ds(part * HALF, HALF)
                power = jnp.exp2(own_scores(h, s, part) * EXP2 - mx[h, s, 0:1, rows]).astype(bf16)
                eo[h, s, :, rows] = power
                acc[h, s, :, rows] = dot(vot[h, s], power)

    @pl.loop(0, NBLOCK)
    def _(j):
        base = pl.multiple_of(j * BLOCK, BLOCK)
        vals = vbuf.at[pl.ds(base, BLOCK)]
        pltpu.make_async_copy(vals, vals, v_recv.at[j]).wait()

        @pl.when(j == 0)
        def _():
            for copy in passing(vbuf, v_send, v_recv):
                copy.start()

        for h in range(HEADS):
            cols = pl.ds(h * HD, HD)
            for n in range(BLOCK // 128):
                vt[h, 0:HD, pl.ds(base + n * 128, 128)] = vbuf[
                    pl.ds(base + n * 128, 128), cols
                ].T
            for s in range(2):
                for part in range(2):
                    rows = pl.ds(part * HALF, HALF)
                    scores = dot(kbuf[pl.ds(base, BLOCK), cols], qt[h, s, :, rows])
                    power = jnp.exp2(scores * EXP2 - mx[h, s, 0:1, rows]).astype(bf16)
                    e[h, j, s, :, rows] = power
                    acc[h, s, :, rows] += dot(vt[h, :, pl.ds(base, BLOCK)], power)

    for step in range(1, 4):
        z_copy(step).wait_recv()
    lens[2, rest] = lens[1, 0] + lens[1, 1] + lens[1, 2] + lens[1, 3]
    for step in range(1, 4):
        rest_copy(step).start()

    def put(src, out, dst_cols, n):
        return (
            pltpu.make_async_copy(src.at[0], out.at[0, :, dst_cols], out_sem.at[n]),
            send(src.at[1], out.at[0, :, dst_cols], out_send.at[n], out_recv.at[n], sibling),
        )

    for s in range(2):
        for h in range(HEADS):
            inv = 1.0 / acc[h, s, HD : HD + 1, :]
            acc[h, s, HD : HD + 1, :] = inv
            cotangent = dot_[h, s].astype(f32)
            total = jnp.sum(acc[h, s, 0:HD, :] * cotangent, axis=0, keepdims=True)
            cen[h, s] = total * inv * inv
            scaled = (cotangent * inv).astype(bf16)
            dot_[h, s] = scaled
            for g in range(GROUP):
                rows = slice(g * ROWS, (g + 1) * ROWS)
                don[h, s, rows, :] = scaled[:, rows].T

    half_rows = BLOCK // 2

    def grad_copy(j, half, n):
        dist = (1 - j) * (1 - 2 * half)
        slot = (y_hi * 2 + core) * 6 + lax.rem(dist + 3, 3) * 2 + y_lo
        to_y = lax.rem(y + n, 4)
        row = pl.multiple_of(j * BLOCK + half * half_rows + to_y * LOCAL, LOCAL)
        return send(
            dkv.at[pl.ds(row, LOCAL)],
            rkv.at[slot],
            grad_send.at[0],
            grad_recv,
            at(lax.rem(z + dist + 4, 4), to_y, half),
        )

    def far_copy(half):
        row = pl.multiple_of(3 * BLOCK + half * half_rows, half_rows)
        return send(
            dkv.at[pl.ds(row, half_rows)],
            far.at[half],
            grad_send.at[1 + half],
            far_recv.at[half],
            at(lax.rem(z + 1 + 2 * half, 4), y, core),
        )


    for h in range(HEADS):
        for s in range(2):
            dq[h, s] = jnp.zeros((HD, CHUNK), f32)

    @pl.loop(0, 2 * NBLOCK)
    def _(step):
        turn = step // 2
        j = (1 - turn // 2) * (3 - turn) + (turn // 2) * (turn - 2)
        half = lax.rem(step + turn * (2 - turn) * (3 - turn) // 2, 2)
        base = pl.multiple_of(j * BLOCK + half * half_rows, half_rows)
        inner = pl.ds(pl.multiple_of(half * half_rows, half_rows), half_rows)
        rows = pl.ds(base, half_rows)
        for h in range(HEADS):
            cols = pl.ds(h * HD, HD)
            dv_part = None
            dk_part = None
            for s in range(2):
                power = e[h, j, s, inner]
                grad = dot(vbuf[rows, cols], dot_[h, s])
                score = (power.astype(f32) * (grad - cen[h, s])).astype(bf16)
                dv_now = dot(power, don[h, s])
                dk_now = dot(score, qn[h, s])
                dv_part = dv_now if s == 0 else dv_part + dv_now
                dk_part = dk_now if s == 0 else dk_part + dk_now
                dq[h, s] += dot(kt[h, :, pl.ds(base, half_rows)], score)
            dkv[rows, pl.ds(h * HD, HD)] = dk_part.astype(bf16)
            dkv[rows, pl.ds(KCOLS + h * HD, HD)] = dv_part.astype(bf16)

        @pl.when(turn == 0)
        def _():
            far_copy(half).start()

        @pl.when(turn == 2)
        def _():
            pltpu.make_async_copy(far.at[half], far.at[half], far_recv.at[half]).wait()
            dkv[rows] = (dkv[rows].astype(f32) + far[half].astype(f32)).astype(bf16)

        @pl.when(turn > 0)
        def _():
            for n in range(4):

                if n == 0:

                    @pl.when(jnp.logical_or(j != 1, half != core))
                    def _():
                        grad_copy(j, half, 0).start()
                else:
                    grad_copy(j, half, n).start()

    pltpu.make_async_copy(
        dkv.at[pl.ds(BLOCK + my_row, LOCAL)], rkv.at[(y_hi * 2 + core) * 6 + y_lo], grad_recv
    ).start()

    for s in range(2):
        live = slot_row < lsum[s, 0:1, :]
        for h in range(HEADS):
            attended = acc[h, s, 0:HD, :] * acc[h, s, HD : HD + 1, :]
            for g in range(GROUP):
                rows = slice(g * ROWS, (g + 1) * ROWS)
                ost[s, :, pl.ds((h * GROUP + g) * HD, HD)] = jnp.where(
                    live, attended[:, rows].T, 0.0
                ).astype(bf16)
    o_copies = put(ost, o_out, my_q, 0)
    o_copies[0].start()
    o_copies[1].start()

    for step in range(1, 4):
        rest_copy(step).wait_recv()
    total = lens[2, 0] + lens[2, 1] + lens[2, 2] + lens[2, 3]
    weight = (4.0 * 16.0 * ROWS) / total[0:1, :]

    for h in range(HEADS):
        cols = pl.ds(h * HD, HD)
        for s in range(2):
            power = eo[h, s]
            grad = dot(vown[s, :, cols], dot_[h, s])
            score = (power.astype(f32) * (grad - cen[h, s])).astype(bf16)
            dvst[s, :, cols] = (dot(power, don[h, s]) * weight).astype(bf16)
            dkst[s, :, cols] = (dot(score, qn[h, s]) * (weight * FACTOR)).astype(bf16)
            dq[h, s] += dot(kot[h, s], score)
    dk_copies = put(dkst, dk_out, my_k, 1)
    dv_copies = put(dvst, dv_out, my_k, 2)
    for copy in dk_copies + dv_copies:
        copy.start()

    for s in range(2):
        for h in range(HEADS):
            for g in range(GROUP):
                rows = slice(g * ROWS, (g + 1) * ROWS)
                dqst[s, :, pl.ds((h * GROUP + g) * HD, HD)] = (
                    dq[h, s, :, rows].T * (weight * FACTOR)
                ).astype(bf16)
    dq_copies = put(dqst, dq_out, my_q, 3)
    for copy in dq_copies:
        copy.start()

    push_done(kbuf, k_send, k_recv)
    push_done(vbuf, v_send, v_recv)
    for copy in pair:
        copy.wait_send()
    for step in range(1, 4):
        x_copy(step).wait_send()
        z_copy(step).wait_send()
        rest_copy(step).wait_send()
    for half in range(2):
        far_copy(half).wait_send()
    for local, remote in (o_copies, dk_copies, dv_copies):
        local.wait()
        remote.wait_send()
        remote.wait_recv()
    sent = dkv.at[pl.ds(0, 23 * LOCAL)]
    pltpu.make_async_copy(sent, sent, grad_send.at[0]).wait()

    pltpu.make_async_copy(rkv, rkv, grad_recv).wait()
    twice = jnp.concatenate([weight, weight], axis=1)
    for n in range(4):
        summed = rkv[n * 6].astype(f32)
        for m in range(1, 6):
            summed += rkv[n * 6 + m].astype(f32)
        cols = slice(n * KCOLS, (n + 1) * KCOLS)
        pkg_out[0, :, cols] = (summed[:, :KCOLS] * (twice * FACTOR)).astype(bf16)
        pvg_out[0, :, cols] = (summed[:, KCOLS:] * twice).astype(bf16)
    dq_copies[0].wait()
    dq_copies[1].wait_send()
    dq_copies[1].wait_recv()


def copy_kernel(*refs):
    sources, results, held, (come, go) = refs[:6], refs[6:12], refs[12:18], refs[18:]
    loads = [pltpu.make_async_copy(sources[n], held[n], come.at[n]) for n in range(6)]
    stores = [pltpu.make_async_copy(held[n], results[n], go.at[n]) for n in range(6)]
    for copy in loads:
        copy.start()
    for n in range(6):
        loads[n].wait()
        stores[n].start()
    for copy in stores:
        copy.wait()


def body(queries, keys, values, prefix_keys, prefix_values, lengths, out_grad):
    vmem = lambda shape, dtype: pltpu.VMEM(shape, dtype)
    dma = pltpu.SemaphoreType.DMA
    prefix = NBLOCK * BLOCK
    anywhere = pl.BlockSpec(memory_space=pl.ANY)
    in_vmem = pl.BlockSpec(memory_space=pltpu.VMEM)
    shape = lambda a: jax.ShapeDtypeStruct(a.shape, bf16)
    results = pl.pallas_call(
        kernel,
        out_shape=[
            shape(queries), shape(queries), shape(keys), shape(values),
            shape(prefix_keys), shape(prefix_values),
        ],
        in_specs=[anywhere] * 5 + [pl.BlockSpec(memory_space=pltpu.SMEM), anywhere],
        out_specs=[anywhere] * 4 + [in_vmem] * 2,
        scratch_shapes=[
            vmem((LOCAL, 8 * HD), bf16), vmem((LOCAL, 8 * HD), bf16),
            vmem((2, ROWS, QCOLS), bf16), vmem((2, ROWS, QCOLS), bf16),
            vmem((2, ROWS, KCOLS), bf16), vmem((2, ROWS, KCOLS), bf16),
            vmem((prefix, KCOLS), bf16), vmem((prefix, KCOLS), bf16),
            vmem((3, 4, 8, 128), f32), vmem((2, 8, 128), f32),
            vmem((HEADS, 2, HD, CHUNK), bf16), vmem((HEADS, 2, CHUNK, HD), bf16),
            vmem((HEADS, 2, HD, CHUNK), bf16), vmem((HEADS, 2, CHUNK, HD), bf16),
            vmem((HEADS, HD + 16, prefix), bf16), vmem((HEADS, HD, prefix), bf16),
            vmem((HEADS, 2, HD, ROWS), bf16), vmem((HEADS, 2, HD + 16, ROWS), bf16),
            vmem((HEADS, NBLOCK, 2, BLOCK, CHUNK), bf16),
            vmem((HEADS, 2, ROWS, CHUNK), bf16),
            vmem((HEADS, 2, 8, CHUNK), f32),
            vmem((HEADS, 2, HD + 16, CHUNK), f32),
            vmem((HEADS, 2, 1, CHUNK), f32),
            vmem((HEADS, 2, HD, CHUNK), f32),
            vmem((2, ROWS, QCOLS), bf16), vmem((2, ROWS, QCOLS), bf16),
            vmem((2, ROWS, KCOLS), bf16), vmem((2, ROWS, KCOLS), bf16),
            vmem((prefix, 2 * KCOLS), bf16),
            vmem((24, LOCAL, 2 * KCOLS), bf16),
            vmem((2, BLOCK // 2, 2 * KCOLS), bf16),
            dma((6,)), dma((5,)), dma((5,)),
            dma((3,)), dma((3,)), dma((NBLOCK,)), dma((NBLOCK,)),
            dma((3, 3)), dma((3, 3)),
            dma((3,)), dma, dma((2,)),
            dma((4,)), dma((4,)), dma((4,)),
        ],
        compiler_params=pltpu.CompilerParams(
            collective_id=0, has_side_effects=True, vmem_limit_bytes=60 * 2**20
        ),
        cost_estimate=pl.CostEstimate(
            flops=14 * 2**30, bytes_accessed=10 * 2**20, transcendentals=9 * 2**20
        ),
    )(queries, keys, values, prefix_keys, prefix_values, lengths, out_grad)
    return pl.pallas_call(
        copy_kernel,
        out_shape=[jax.ShapeDtypeStruct(a.shape, a.dtype) for a in results],
        in_specs=[anywhere] * 6,
        out_specs=[anywhere] * 6,
        scratch_shapes=[vmem(a.shape, a.dtype) for a in results] + [dma((6,)), dma((6,))],
    )(*results)


def solution(mesh):
    in_specs = (
        P("prompt", "response", "tensor"),
        P("prompt", "response", "tensor"),
        P("prompt", "response", "tensor"),
        P("prompt", ("response", "tensor"), None),
        P("prompt", ("response", "tensor"), None),
        P("prompt", "response"),
        P("prompt", "response", "tensor"),
    )
    out_specs = (
        P("prompt", "response", "tensor"),
        P("prompt", "response", "tensor"),
        P("prompt", "response", "tensor"),
        P("prompt", "response", "tensor"),
        P("prompt", ("response", "tensor"), None),
        P("prompt", ("response", "tensor"), None),
    )
    return jax.shard_map(body, mesh=mesh, in_specs=in_specs, out_specs=out_specs, check_vma=False)
```

```python
import math

import jax
import jax.numpy as jnp
from jax import lax
from jax.experimental import pallas as pl
from jax.experimental.pallas import tpu as pltpu
from jax.sharding import PartitionSpec as P

HD = 128
GROUP = 8
ROWS = 128
LOCAL = 64
BLOCK = 512
NBLOCK = 4
CHUNK = 1024
HALF = 1024
HEADS = 2
QCOLS = HEADS * GROUP * HD
KCOLS = HEADS * HD
FACTOR = 1.0 / math.sqrt(HD)
EXP2 = math.log2(math.e) * FACTOR
MESH = pl.DeviceIdType.MESH
f32 = jnp.float32
bf16 = jnp.bfloat16


def dot(a, b):
    return jnp.dot(a, b, preferred_element_type=f32)


def kernel(
    q_in, k_in, v_in, pk_in, pv_in, len_in, do_in,
    o_out, dq_out, dk_out, dv_out, pkg_out, pvg_out,
    pk, pv, qin, din, kown, vown, kbuf, vbuf, lens, lsum,
    qt, qn, dot_, don, vt, kt, kot, vot, e, eo, mx, acc, cen, dq,
    ost, dqst, dkst, dvst, dkv, rkv, far,
    load_sem, pair_send, pair_recv, k_send, v_send, k_recv, v_recv,
    len_send, len_recv, grad_send, grad_recv, far_recv, out_send, out_recv, out_sem,
):
    prompt = lax.axis_index("prompt")
    resp = lax.axis_index("response")
    y_hi = lax.axis_index("tensor")
    core = lax.rem(resp, 2)
    z = lax.rem(resp // 2, 4)
    y_lo = resp // 8
    y = y_hi * 2 + y_lo
    other = 1 - core

    def at(zz, yy, cc):
        return {"response": lax.rem(yy, 2) * 8 + zz * 2 + cc, "tensor": yy // 2}

    def along_x(pp):
        return {"prompt": pp}

    sibling = {"response": resp + 1 - 2 * core}
    my_q = pl.ds(pl.multiple_of(core * QCOLS, QCOLS), QCOLS)
    its_q = pl.ds(pl.multiple_of(other * QCOLS, QCOLS), QCOLS)
    my_k = pl.ds(pl.multiple_of(core * KCOLS, KCOLS), KCOLS)
    its_k = pl.ds(pl.multiple_of(other * KCOLS, KCOLS), KCOLS)

    loads = [
        pltpu.make_async_copy(pk_in.at[0], pk, load_sem.at[0]),
        pltpu.make_async_copy(pv_in.at[0], pv, load_sem.at[1]),
        pltpu.make_async_copy(q_in.at[0, :, my_q], qin.at[0], load_sem.at[2]),
        pltpu.make_async_copy(do_in.at[0, :, my_q], din.at[0], load_sem.at[3]),
        pltpu.make_async_copy(k_in.at[0, :, my_k], kown.at[0], load_sem.at[4]),
        pltpu.make_async_copy(v_in.at[0, :, my_k], vown.at[0], load_sem.at[5]),
    ]
    for copy in loads:
        copy.start()

    barrier = pltpu.get_barrier_semaphore()

    def greet(device):
        pl.semaphore_signal(barrier, inc=1, device_id=device, device_id_type=MESH)

    for dist in (1, 3, 0):
        for n in range(8):
            if dist or n:
                greet(
                    at(
                        lax.rem(z + dist, 4),
                        lax.rem(y + n // 2, 4),
                        lax.rem(core + n % 2, 2),
                    )
                )
    greet(at(lax.rem(z + 2, 4), y, core))
    for step in range(1, 4):
        greet(along_x(lax.rem(prompt + step, 4)))
    pl.semaphore_wait(barrier, 27)

    def send(src, dst, send_sem, recv_sem, device):
        return pltpu.make_async_remote_copy(
            src_ref=src,
            dst_ref=dst,
            send_sem=send_sem,
            recv_sem=recv_sem,
            device_id=device,
            device_id_type=MESH,
        )

    lens[0, prompt] = jnp.full((8, 128), len_in[0, 0], jnp.int32).astype(f32)
    pair = [
        send(lens.at[0, prompt], lsum.at[1], pair_send.at[0], pair_recv.at[0], sibling),
        send(q_in.at[0, :, its_q], qin.at[1], pair_send.at[1], pair_recv.at[1], sibling),
        send(k_in.at[0, :, its_k], kown.at[1], pair_send.at[2], pair_recv.at[2], sibling),
        send(do_in.at[0, :, its_q], din.at[1], pair_send.at[3], pair_recv.at[3], sibling),
        send(v_in.at[0, :, its_k], vown.at[1], pair_send.at[4], pair_recv.at[4], sibling),
    ]
    lsum[0] = lens[0, prompt]
    pair[0].start()
    pair[1].start()
    pair[2].start()

    my_row = pl.multiple_of((core * 4 + y) * LOCAL, LOCAL)
    up, down = lax.rem(z + 1, 4), lax.rem(z + 3, 4)
    routes = ((0, lax.rem(z + 3 + 2 * core, 4)), (1, z), (2, lax.rem(z + 5 - 2 * core, 4)))

    def push(shard, buf, send_sems, recv_sems):
        for block, to_z in routes:
            for n in range(8):
                if block == 1 and n == 0:
                    continue
                to_y = lax.rem(y + n // 2, 4)
                to_core = lax.rem(core + n % 2, 2)
                cols = pl.multiple_of(((to_y // 2) * 2 + to_core) * KCOLS, KCOLS)
                send(
                    shard.at[:, pl.ds(cols, KCOLS)],
                    buf.at[pl.ds(block * BLOCK + my_row, LOCAL)],
                    send_sems.at[0],
                    recv_sems.at[block],
                    at(to_z, to_y, to_core),
                ).start()

    def passing(buf, send_sems, recv_sems):
        half = BLOCK // 2
        return [
            send(
                buf.at[pl.ds(n * half, half)],
                buf.at[pl.ds(3 * BLOCK + n * half, half)],
                send_sems.at[1 + n],
                recv_sems.at[3],
                at(down if n == 0 else up, y, core),
            )
            for n in range(2)
        ]

    def push_done(buf, send_sems, recv_sems):
        sent = buf.at[pl.ds(0, 23 * LOCAL)]
        pltpu.make_async_copy(sent, sent, send_sems.at[0]).wait()
        for copy in passing(buf, send_sems, recv_sems):
            copy.wait_send()

    mine = pl.ds(pl.multiple_of((y_hi * 2 + core) * KCOLS, KCOLS), KCOLS)
    loads[0].wait()
    push(pk, kbuf, k_send, k_recv)
    pltpu.make_async_copy(pk.at[:, mine], kbuf.at[pl.ds(BLOCK + my_row, LOCAL)], k_recv.at[1]).start()
    pair[3].start()
    pair[4].start()
    loads[1].wait()
    pltpu.make_async_copy(pv.at[:, mine], vbuf.at[pl.ds(BLOCK + my_row, LOCAL)], v_recv.at[1]).start()

    def x_copy(step):
        return send(
            lens.at[0, prompt], lens.at[0, prompt], len_send.at[0, step - 1],
            len_recv.at[0, step - 1], along_x(lax.rem(prompt + step, 4)),
        )

    def z_copy(step):
        return send(
            lens.at[1, z], lens.at[1, z], len_send.at[1, step - 1],
            len_recv.at[1, step - 1], at(lax.rem(z + step, 4), y, core),
        )

    rest = y_lo * 2 + core

    def rest_copy(step):
        slot = lax.rem(rest + step, 4)
        return send(
            lens.at[2, rest], lens.at[2, rest], len_send.at[2, step - 1],
            len_recv.at[2, step - 1], at(z, y_hi * 2 + slot // 2, lax.rem(slot, 2)),
        )

    for step in range(1, 4):
        x_copy(step).start()

    slot_row = lax.broadcasted_iota(jnp.int32, (ROWS, HD), 0).astype(f32)

    def stage_q(s):
        for h in range(HEADS):
            for g in range(GROUP):
                cols = pl.ds((h * GROUP + g) * HD, HD)
                block = qin[s, :, cols]
                qn[h, s, g * ROWS : (g + 1) * ROWS, :] = block
                qt[h, s, :, g * ROWS : (g + 1) * ROWS] = block.T

    def stage_do(s):
        live = slot_row < lsum[s, 0:1, :]
        for h in range(HEADS):
            for g in range(GROUP):
                cols = pl.ds((h * GROUP + g) * HD, HD)
                block = jnp.where(live, din[s, :, cols].astype(f32), 0.0).astype(bf16)
                dot_[h, s, :, g * ROWS : (g + 1) * ROWS] = block.T

    def stage_own(s):
        for h in range(HEADS):
            cols = pl.ds(h * HD, HD)
            kot[h, s] = kown[s, :, cols].T
            vot[h, s, 0:HD] = vown[s, :, cols].T
            vot[h, s, HD : HD + 16] = jnp.ones((16, ROWS), bf16)

    allowed = lax.broadcasted_iota(jnp.int32, (ROWS, HALF), 0) <= lax.rem(
        lax.broadcasted_iota(jnp.int32, (ROWS, HALF), 1), ROWS
    )

    def own_scores(h, s, part):
        scores = dot(kown[s, :, pl.ds(h * HD, HD)], qt[h, s, :, part * HALF : (part + 1) * HALF])
        return jnp.where(allowed, scores, -1e30)

    def own_max(s):
        for h in range(HEADS):
            for part in range(CHUNK // HALF):
                cols = pl.ds(part * HALF, HALF)
                mx[h, s, :, cols] = jnp.max(
                    own_scores(h, s, part).reshape(ROWS // 8, 8, HALF), axis=0
                )

    loads[2].wait()
    loads[4].wait()
    stage_q(0)
    own_max(0)
    loads[3].wait()
    stage_do(0)
    loads[5].wait()
    stage_own(0)
    for h in range(HEADS):
        vt[h, HD : HD + 16] = jnp.ones((16, NBLOCK * BLOCK), bf16)
    pair[0].wait_recv()
    pair[1].wait_recv()
    pair[2].wait_recv()
    stage_q(1)
    own_max(1)

    push(pv, vbuf, v_send, v_recv)
    @pl.loop(0, NBLOCK)
    def _(j):
        base = pl.multiple_of(j * BLOCK, BLOCK)
        keys = kbuf.at[pl.ds(base, BLOCK)]
        pltpu.make_async_copy(keys, keys, k_recv.at[j]).wait()

        @pl.when(j == 0)
        def _():
            for copy in passing(kbuf, k_send, k_recv):
                copy.start()

        for h in range(HEADS):
            cols = pl.ds(h * HD, HD)
            for n in range(BLOCK // 128):
                kt[h, :, pl.ds(base + n * 128, 128)] = kbuf[pl.ds(base + n * 128, 128), cols].T
            for s in range(2):
                for part in range(CHUNK // HALF):
                    rows = pl.ds(part * HALF, HALF)
                    scores = dot(kbuf[pl.ds(base, BLOCK), cols], qt[h, s, :, rows])
                    mx[h, s, :, rows] = jnp.maximum(
                        mx[h, s, :, rows],
                        jnp.max(scores.reshape(BLOCK // 8, 8, HALF), axis=0),
                    )

    for step in range(1, 4):
        x_copy(step).wait_recv()
    lens[1, z] = lens[0, 0] + lens[0, 1] + lens[0, 2] + lens[0, 3]
    for step in range(1, 4):
        z_copy(step).start()

    pair[3].wait_recv()
    pair[4].wait_recv()
    stage_do(1)
    stage_own(1)

    for h in range(HEADS):
        for s in range(2):
            top = jnp.max(mx[h, s], axis=0, keepdims=True) * EXP2
            mx[h, s] = jnp.broadcast_to(top, (8, CHUNK))
            for part in range(CHUNK // HALF):
                rows = pl.ds(part * HALF, HALF)
                power = jnp.exp2(own_scores(h, s, part) * EXP2 - mx[h, s, 0:1, rows]).astype(bf16)
                eo[h, s, :, rows] = power
                acc[h, s, :, rows] = dot(vot[h, s], power)

    @pl.loop(0, NBLOCK)
    def _(j):
        base = pl.multiple_of(j * BLOCK, BLOCK)
        vals = vbuf.at[pl.ds(base, BLOCK)]
        pltpu.make_async_copy(vals, vals, v_recv.at[j]).wait()

        @pl.when(j == 0)
        def _():
            for copy in passing(vbuf, v_send, v_recv):
                copy.start()

        for h in range(HEADS):
            cols = pl.ds(h * HD, HD)
            for n in range(BLOCK // 128):
                vt[h, 0:HD, pl.ds(base + n * 128, 128)] = vbuf[
                    pl.ds(base + n * 128, 128), cols
                ].T
            for s in range(2):
                for part in range(CHUNK // HALF):
                    rows = pl.ds(part * HALF, HALF)
                    scores = dot(kbuf[pl.ds(base, BLOCK), cols], qt[h, s, :, rows])
                    power = jnp.exp2(scores * EXP2 - mx[h, s, 0:1, rows]).astype(bf16)
                    e[h, j, s, :, rows] = power
                    acc[h, s, :, rows] += dot(vt[h, :, pl.ds(base, BLOCK)], power)

    for step in range(1, 4):
        z_copy(step).wait_recv()
    lens[2, rest] = lens[1, 0] + lens[1, 1] + lens[1, 2] + lens[1, 3]
    for step in range(1, 4):
        rest_copy(step).start()

    def put(src, out, dst_cols, n):
        return (
            pltpu.make_async_copy(src.at[0], out.at[0, :, dst_cols], out_sem.at[n]),
            send(src.at[1], out.at[0, :, dst_cols], out_send.at[n], out_recv.at[n], sibling),
        )

    for s in range(2):
        for h in range(HEADS):
            inv = 1.0 / acc[h, s, HD : HD + 1, :]
            acc[h, s, HD : HD + 1, :] = inv
            cotangent = dot_[h, s].astype(f32)
            total = jnp.sum(acc[h, s, 0:HD, :] * cotangent, axis=0, keepdims=True)
            cen[h, s] = total * inv * inv
            scaled = (cotangent * inv).astype(bf16)
            dot_[h, s] = scaled
            for g in range(GROUP):
                rows = slice(g * ROWS, (g + 1) * ROWS)
                don[h, s, rows, :] = scaled[:, rows].T

    half_rows = BLOCK // 2

    def grad_copy(j, half, n):
        dist = (1 - j) * (1 - 2 * half)
        slot = (y_hi * 2 + core) * 6 + lax.rem(dist + 3, 3) * 2 + y_lo
        to_y = lax.rem(y + n, 4)
        row = pl.multiple_of(j * BLOCK + half * half_rows + to_y * LOCAL, LOCAL)
        return send(
            dkv.at[pl.ds(row, LOCAL)],
            rkv.at[slot],
            grad_send.at[0],
            grad_recv,
            at(lax.rem(z + dist + 4, 4), to_y, half),
        )

    def far_copy(half):
        row = pl.multiple_of(3 * BLOCK + half * half_rows, half_rows)
        return send(
            dkv.at[pl.ds(row, half_rows)],
            far.at[half],
            grad_send.at[1 + half],
            far_recv.at[half],
            at(lax.rem(z + 1 + 2 * half, 4), y, core),
        )


    for h in range(HEADS):
        for s in range(2):
            dq[h, s] = jnp.zeros((HD, CHUNK), f32)

    @pl.loop(0, 2 * NBLOCK)
    def _(step):
        turn = step // 2
        j = (1 - turn // 2) * (3 - turn) + (turn // 2) * (turn - 2)
        half = lax.rem(step + turn * (2 - turn) * (3 - turn) // 2, 2)
        base = pl.multiple_of(j * BLOCK + half * half_rows, half_rows)
        inner = pl.ds(pl.multiple_of(half * half_rows, half_rows), half_rows)
        rows = pl.ds(base, half_rows)
        for h in range(HEADS):
            cols = pl.ds(h * HD, HD)
            dv_part = None
            dk_part = None
            for s in range(2):
                power = e[h, j, s, inner]
                grad = dot(vbuf[rows, cols], dot_[h, s])
                score = (power.astype(f32) * (grad - cen[h, s])).astype(bf16)
                dv_now = dot(power, don[h, s])
                dk_now = dot(score, qn[h, s])
                dv_part = dv_now if s == 0 else dv_part + dv_now
                dk_part = dk_now if s == 0 else dk_part + dk_now
                dq[h, s] += dot(kt[h, :, pl.ds(base, half_rows)], score)
            dkv[rows, pl.ds(h * HD, HD)] = dk_part.astype(bf16)
            dkv[rows, pl.ds(KCOLS + h * HD, HD)] = dv_part.astype(bf16)

        @pl.when(turn == 0)
        def _():
            far_copy(half).start()

        @pl.when(turn == 2)
        def _():
            pltpu.make_async_copy(far.at[half], far.at[half], far_recv.at[half]).wait()
            dkv[rows] = (dkv[rows].astype(f32) + far[half].astype(f32)).astype(bf16)

        @pl.when(turn > 0)
        def _():
            for n in range(4):

                if n == 0:

                    @pl.when(jnp.logical_or(j != 1, half != core))
                    def _():
                        grad_copy(j, half, 0).start()
                else:
                    grad_copy(j, half, n).start()

    pltpu.make_async_copy(
        dkv.at[pl.ds(BLOCK + my_row, LOCAL)], rkv.at[(y_hi * 2 + core) * 6 + y_lo], grad_recv
    ).start()

    for s in range(2):
        live = slot_row < lsum[s, 0:1, :]
        for h in range(HEADS):
            attended = acc[h, s, 0:HD, :] * acc[h, s, HD : HD + 1, :]
            for g in range(GROUP):
                rows = slice(g * ROWS, (g + 1) * ROWS)
                ost[s, :, pl.ds((h * GROUP + g) * HD, HD)] = jnp.where(
                    live, attended[:, rows].T, 0.0
                ).astype(bf16)
    o_copies = put(ost, o_out, my_q, 0)
    o_copies[0].start()
    o_copies[1].start()

    for step in range(1, 4):
        rest_copy(step).wait_recv()
    total = lens[2, 0] + lens[2, 1] + lens[2, 2] + lens[2, 3]
    weight = (4.0 * 16.0 * ROWS) / total[0:1, :]

    for h in range(HEADS):
        cols = pl.ds(h * HD, HD)
        for s in range(2):
            power = eo[h, s]
            grad = dot(vown[s, :, cols], dot_[h, s])
            score = (power.astype(f32) * (grad - cen[h, s])).astype(bf16)
            dvst[s, :, cols] = (dot(power, don[h, s]) * weight).astype(bf16)
            dkst[s, :, cols] = (dot(score, qn[h, s]) * (weight * FACTOR)).astype(bf16)
            dq[h, s] += dot(kot[h, s], score)
    dk_copies = put(dkst, dk_out, my_k, 1)
    dv_copies = put(dvst, dv_out, my_k, 2)
    for copy in dk_copies + dv_copies:
        copy.start()

    for s in range(2):
        for h in range(HEADS):
            for g in range(GROUP):
                rows = slice(g * ROWS, (g + 1) * ROWS)
                dqst[s, :, pl.ds((h * GROUP + g) * HD, HD)] = (
                    dq[h, s, :, rows].T * (weight * FACTOR)
                ).astype(bf16)
    dq_copies = put(dqst, dq_out, my_q, 3)
    for copy in dq_copies:
        copy.start()

    push_done(kbuf, k_send, k_recv)
    push_done(vbuf, v_send, v_recv)
    for copy in pair:
        copy.wait_send()
    for step in range(1, 4):
        x_copy(step).wait_send()
        z_copy(step).wait_send()
        rest_copy(step).wait_send()
    for half in range(2):
        far_copy(half).wait_send()
    for local, remote in (o_copies, dk_copies, dv_copies):
        local.wait()
        remote.wait_send()
        remote.wait_recv()
    sent = dkv.at[pl.ds(0, 23 * LOCAL)]
    pltpu.make_async_copy(sent, sent, grad_send.at[0]).wait()

    pltpu.make_async_copy(rkv, rkv, grad_recv).wait()
    twice = jnp.concatenate([weight, weight], axis=1)
    for n in range(4):
        summed = rkv[n * 6].astype(f32)
        for m in range(1, 6):
            summed += rkv[n * 6 + m].astype(f32)
        cols = slice(n * KCOLS, (n + 1) * KCOLS)
        pkg_out[0, :, cols] = (summed[:, :KCOLS] * (twice * FACTOR)).astype(bf16)
        pvg_out[0, :, cols] = (summed[:, KCOLS:] * twice).astype(bf16)
    dq_copies[0].wait()
    dq_copies[1].wait_send()
    dq_copies[1].wait_recv()


def copy_kernel(*refs):
    sources, results, held, (come, go) = refs[:6], refs[6:12], refs[12:18], refs[18:]
    loads = [pltpu.make_async_copy(sources[n], held[n], come.at[n]) for n in range(6)]
    stores = [pltpu.make_async_copy(held[n], results[n], go.at[n]) for n in range(6)]
    for copy in loads:
        copy.start()
    for n in range(6):
        loads[n].wait()
        stores[n].start()
    for copy in stores:
        copy.wait()


def body(queries, keys, values, prefix_keys, prefix_values, lengths, out_grad):
    vmem = lambda shape, dtype: pltpu.VMEM(shape, dtype)
    dma = pltpu.SemaphoreType.DMA
    prefix = NBLOCK * BLOCK
    anywhere = pl.BlockSpec(memory_space=pl.ANY)
    in_vmem = pl.BlockSpec(memory_space=pltpu.VMEM)
    shape = lambda a: jax.ShapeDtypeStruct(a.shape, bf16)
    results = pl.pallas_call(
        kernel,
        out_shape=[
            shape(queries), shape(queries), shape(keys), shape(values),
            shape(prefix_keys), shape(prefix_values),
        ],
        in_specs=[anywhere] * 5 + [pl.BlockSpec(memory_space=pltpu.SMEM), anywhere],
        out_specs=[anywhere] * 4 + [in_vmem] * 2,
        scratch_shapes=[
            vmem((LOCAL, 8 * HD), bf16), vmem((LOCAL, 8 * HD), bf16),
            vmem((2, ROWS, QCOLS), bf16), vmem((2, ROWS, QCOLS), bf16),
            vmem((2, ROWS, KCOLS), bf16), vmem((2, ROWS, KCOLS), bf16),
            vmem((prefix, KCOLS), bf16), vmem((prefix, KCOLS), bf16),
            vmem((3, 4, 8, 128), f32), vmem((2, 8, 128), f32),
            vmem((HEADS, 2, HD, CHUNK), bf16), vmem((HEADS, 2, CHUNK, HD), bf16),
            vmem((HEADS, 2, HD, CHUNK), bf16), vmem((HEADS, 2, CHUNK, HD), bf16),
            vmem((HEADS, HD + 16, prefix), bf16), vmem((HEADS, HD, prefix), bf16),
            vmem((HEADS, 2, HD, ROWS), bf16), vmem((HEADS, 2, HD + 16, ROWS), bf16),
            vmem((HEADS, NBLOCK, 2, BLOCK, CHUNK), bf16),
            vmem((HEADS, 2, ROWS, CHUNK), bf16),
            vmem((HEADS, 2, 8, CHUNK), f32),
            vmem((HEADS, 2, HD + 16, CHUNK), f32),
            vmem((HEADS, 2, 1, CHUNK), f32),
            vmem((HEADS, 2, HD, CHUNK), f32),
            vmem((2, ROWS, QCOLS), bf16), vmem((2, ROWS, QCOLS), bf16),
            vmem((2, ROWS, KCOLS), bf16), vmem((2, ROWS, KCOLS), bf16),
            vmem((prefix, 2 * KCOLS), bf16),
            vmem((24, LOCAL, 2 * KCOLS), bf16),
            vmem((2, BLOCK // 2, 2 * KCOLS), bf16),
            dma((6,)), dma((5,)), dma((5,)),
            dma((3,)), dma((3,)), dma((NBLOCK,)), dma((NBLOCK,)),
            dma((3, 3)), dma((3, 3)),
            dma((3,)), dma, dma((2,)),
            dma((4,)), dma((4,)), dma((4,)),
        ],
        compiler_params=pltpu.CompilerParams(
            collective_id=0, has_side_effects=True, vmem_limit_bytes=60 * 2**20
        ),
        cost_estimate=pl.CostEstimate(
            flops=14 * 2**30, bytes_accessed=10 * 2**20, transcendentals=9 * 2**20
        ),
    )(queries, keys, values, prefix_keys, prefix_values, lengths, out_grad)
    return pl.pallas_call(
        copy_kernel,
        out_shape=[jax.ShapeDtypeStruct(a.shape, a.dtype) for a in results],
        in_specs=[anywhere] * 6,
        out_specs=[anywhere] * 6,
        scratch_shapes=[vmem(a.shape, a.dtype) for a in results] + [dma((6,)), dma((6,))],
    )(*results)


def solution(mesh):
    in_specs = (
        P("prompt", "response", "tensor"),
        P("prompt", "response", "tensor"),
        P("prompt", "response", "tensor"),
        P("prompt", ("response", "tensor"), None),
        P("prompt", ("response", "tensor"), None),
        P("prompt", "response"),
        P("prompt", "response", "tensor"),
    )
    out_specs = (
        P("prompt", "response", "tensor"),
        P("prompt", "response", "tensor"),
        P("prompt", "response", "tensor"),
        P("prompt", "response", "tensor"),
        P("prompt", ("response", "tensor"), None),
        P("prompt", ("response", "tensor"), None),
    )
    return jax.shard_map(body, mesh=mesh, in_specs=in_specs, out_specs=out_specs, check_vma=False)
```

```python
import math

import jax
import jax.numpy as jnp
from jax import lax
from jax.experimental import pallas as pl
from jax.experimental.pallas import tpu as pltpu
from jax.sharding import PartitionSpec as P

HD = 128
GROUP = 8
ROWS = 128
LOCAL = 64
BLOCK = 512
NBLOCK = 4
CHUNK = 1024
HALF = 1024
HEADS = 2
QCOLS = HEADS * GROUP * HD
KCOLS = HEADS * HD
FACTOR = 1.0 / math.sqrt(HD)
EXP2 = math.log2(math.e) * FACTOR
MESH = pl.DeviceIdType.MESH
f32 = jnp.float32
bf16 = jnp.bfloat16


def dot(a, b):
    return jnp.dot(a, b, preferred_element_type=f32)


def kernel(
    q_in, k_in, v_in, pk_in, pv_in, len_in, do_in,
    o_out, dq_out, dk_out, dv_out, pkg_out, pvg_out,
    pk, pv, qin, din, kown, vown, kbuf, vbuf, lens, lsum,
    qt, qn, dot_, don, vt, kt, kot, vot, e, eo, mx, acc, cen, dq,
    ost, dqst, dkst, dvst, dkv, rkv, far,
    load_sem, pair_send, pair_recv, k_send, v_send, k_recv, v_recv,
    len_send, len_recv, grad_send, grad_recv, far_recv, out_send, out_recv, out_sem,
):
    prompt = lax.axis_index("prompt")
    resp = lax.axis_index("response")
    y_hi = lax.axis_index("tensor")
    core = lax.rem(resp, 2)
    z = lax.rem(resp // 2, 4)
    y_lo = resp // 8
    y = y_hi * 2 + y_lo
    other = 1 - core

    def at(zz, yy, cc):
        return {"response": lax.rem(yy, 2) * 8 + zz * 2 + cc, "tensor": yy // 2}

    def along_x(pp):
        return {"prompt": pp}

    sibling = {"response": resp + 1 - 2 * core}
    my_q = pl.ds(pl.multiple_of(core * QCOLS, QCOLS), QCOLS)
    its_q = pl.ds(pl.multiple_of(other * QCOLS, QCOLS), QCOLS)
    my_k = pl.ds(pl.multiple_of(core * KCOLS, KCOLS), KCOLS)
    its_k = pl.ds(pl.multiple_of(other * KCOLS, KCOLS), KCOLS)

    loads = [
        pltpu.make_async_copy(pk_in.at[0], pk, load_sem.at[0]),
        pltpu.make_async_copy(pv_in.at[0], pv, load_sem.at[1]),
        pltpu.make_async_copy(q_in.at[0, :, my_q], qin.at[0], load_sem.at[2]),
        pltpu.make_async_copy(do_in.at[0, :, my_q], din.at[0], load_sem.at[3]),
        pltpu.make_async_copy(k_in.at[0, :, my_k], kown.at[0], load_sem.at[4]),
        pltpu.make_async_copy(v_in.at[0, :, my_k], vown.at[0], load_sem.at[5]),
    ]
    for copy in loads:
        copy.start()

    barrier = pltpu.get_barrier_semaphore()

    def greet(device):
        pl.semaphore_signal(barrier, inc=1, device_id=device, device_id_type=MESH)

    for dist in (1, 3, 0):
        for n in range(8):
            if dist or n:
                greet(
                    at(
                        lax.rem(z + dist, 4),
                        lax.rem(y + n // 2, 4),
                        lax.rem(core + n % 2, 2),
                    )
                )
    greet(at(lax.rem(z + 2, 4), y, core))
    for step in range(1, 4):
        greet(along_x(lax.rem(prompt + step, 4)))
    pl.semaphore_wait(barrier, 27)

    def send(src, dst, send_sem, recv_sem, device):
        return pltpu.make_async_remote_copy(
            src_ref=src,
            dst_ref=dst,
            send_sem=send_sem,
            recv_sem=recv_sem,
            device_id=device,
            device_id_type=MESH,
        )

    lens[0, prompt] = jnp.full((8, 128), len_in[0, 0], jnp.int32).astype(f32)
    pair = [
        send(lens.at[0, prompt], lsum.at[1], pair_send.at[0], pair_recv.at[0], sibling),
        send(q_in.at[0, :, its_q], qin.at[1], pair_send.at[1], pair_recv.at[1], sibling),
        send(k_in.at[0, :, its_k], kown.at[1], pair_send.at[2], pair_recv.at[2], sibling),
        send(do_in.at[0, :, its_q], din.at[1], pair_send.at[3], pair_recv.at[3], sibling),
        send(v_in.at[0, :, its_k], vown.at[1], pair_send.at[4], pair_recv.at[4], sibling),
    ]
    lsum[0] = lens[0, prompt]
    pair[0].start()
    pair[1].start()
    pair[2].start()

    my_row = pl.multiple_of((core * 4 + y) * LOCAL, LOCAL)
    up, down = lax.rem(z + 1, 4), lax.rem(z + 3, 4)
    routes = ((0, lax.rem(z + 3 + 2 * core, 4)), (1, z), (2, lax.rem(z + 5 - 2 * core, 4)))

    def push(shard, buf, send_sems, recv_sems):
        for block, to_z in routes:
            for n in range(8):
                if block == 1 and n == 0:
                    continue
                to_y = lax.rem(y + n // 2, 4)
                to_core = lax.rem(core + n % 2, 2)
                cols = pl.multiple_of(((to_y // 2) * 2 + to_core) * KCOLS, KCOLS)
                send(
                    shard.at[:, pl.ds(cols, KCOLS)],
                    buf.at[pl.ds(block * BLOCK + my_row, LOCAL)],
                    send_sems.at[0],
                    recv_sems.at[block],
                    at(to_z, to_y, to_core),
                ).start()

    def passing(buf, send_sems, recv_sems):
        half = BLOCK // 2
        return [
            send(
                buf.at[pl.ds(n * half, half)],
                buf.at[pl.ds(3 * BLOCK + n * half, half)],
                send_sems.at[1 + n],
                recv_sems.at[3],
                at(down if n == 0 else up, y, core),
            )
            for n in range(2)
        ]

    def push_done(buf, send_sems, recv_sems):
        sent = buf.at[pl.ds(0, 23 * LOCAL)]
        pltpu.make_async_copy(sent, sent, send_sems.at[0]).wait()
        for copy in passing(buf, send_sems, recv_sems):
            copy.wait_send()

    mine = pl.ds(pl.multiple_of((y_hi * 2 + core) * KCOLS, KCOLS), KCOLS)
    loads[0].wait()
    push(pk, kbuf, k_send, k_recv)
    pltpu.make_async_copy(pk.at[:, mine], kbuf.at[pl.ds(BLOCK + my_row, LOCAL)], k_recv.at[1]).start()
    pair[3].start()
    pair[4].start()
    loads[1].wait()
    pltpu.make_async_copy(pv.at[:, mine], vbuf.at[pl.ds(BLOCK + my_row, LOCAL)], v_recv.at[1]).start()

    def x_copy(step):
        return send(
            lens.at[0, prompt], lens.at[0, prompt], len_send.at[0, step - 1],
            len_recv.at[0, step - 1], along_x(lax.rem(prompt + step, 4)),
        )

    def z_copy(step):
        return send(
            lens.at[1, z], lens.at[1, z], len_send.at[1, step - 1],
            len_recv.at[1, step - 1], at(lax.rem(z + step, 4), y, core),
        )

    rest = y_lo * 2 + core

    def rest_copy(step):
        slot = lax.rem(rest + step, 4)
        return send(
            lens.at[2, rest], lens.at[2, rest], len_send.at[2, step - 1],
            len_recv.at[2, step - 1], at(z, y_hi * 2 + slot // 2, lax.rem(slot, 2)),
        )

    for step in range(1, 4):
        x_copy(step).start()

    slot_row = lax.broadcasted_iota(jnp.int32, (ROWS, HD), 0).astype(f32)

    def stage_q(s):
        for h in range(HEADS):
            for g in range(GROUP):
                cols = pl.ds((h * GROUP + g) * HD, HD)
                block = qin[s, :, cols]
                qn[h, s, g * ROWS : (g + 1) * ROWS, :] = block
                qt[h, s, :, g * ROWS : (g + 1) * ROWS] = block.T

    def stage_do(s):
        live = slot_row < lsum[s, 0:1, :]
        for h in range(HEADS):
            for g in range(GROUP):
                cols = pl.ds((h * GROUP + g) * HD, HD)
                block = jnp.where(live, din[s, :, cols].astype(f32), 0.0).astype(bf16)
                dot_[h, s, :, g * ROWS : (g + 1) * ROWS] = block.T

    def stage_own(s):
        for h in range(HEADS):
            cols = pl.ds(h * HD, HD)
            kot[h, s] = kown[s, :, cols].T
            vot[h, s, 0:HD] = vown[s, :, cols].T
            vot[h, s, HD : HD + 16] = jnp.ones((16, ROWS), bf16)

    allowed = lax.broadcasted_iota(jnp.int32, (ROWS, HALF), 0) <= lax.rem(
        lax.broadcasted_iota(jnp.int32, (ROWS, HALF), 1), ROWS
    )

    def own_scores(h, s, part):
        scores = dot(kown[s, :, pl.ds(h * HD, HD)], qt[h, s, :, part * HALF : (part + 1) * HALF])
        return jnp.where(allowed, scores, -1e30)

    def own_max(s):
        for h in range(HEADS):
            for part in range(CHUNK // HALF):
                cols = pl.ds(part * HALF, HALF)
                mx[h, s, :, cols] = jnp.max(
                    own_scores(h, s, part).reshape(ROWS // 8, 8, HALF), axis=0
                )

    loads[2].wait()
    loads[4].wait()
    stage_q(0)
    own_max(0)
    loads[3].wait()
    stage_do(0)
    loads[5].wait()
    stage_own(0)
    for h in range(HEADS):
        vt[h, HD : HD + 16] = jnp.ones((16, NBLOCK * BLOCK), bf16)
    pair[0].wait_recv()
    pair[1].wait_recv()
    pair[2].wait_recv()
    stage_q(1)
    own_max(1)

    push(pv, vbuf, v_send, v_recv)
    @pl.loop(0, NBLOCK)
    def _(j):
        base = pl.multiple_of(j * BLOCK, BLOCK)
        keys = kbuf.at[pl.ds(base, BLOCK)]
        pltpu.make_async_copy(keys, keys, k_recv.at[j]).wait()

        @pl.when(j == 0)
        def _():
            for copy in passing(kbuf, k_send, k_recv):
                copy.start()

        for h in range(HEADS):
            cols = pl.ds(h * HD, HD)
            for n in range(BLOCK // 128):
                kt[h, :, pl.ds(base + n * 128, 128)] = kbuf[pl.ds(base + n * 128, 128), cols].T
            for s in range(2):
                for part in range(CHUNK // HALF):
                    rows = pl.ds(part * HALF, HALF)
                    scores = dot(kbuf[pl.ds(base, BLOCK), cols], qt[h, s, :, rows])
                    mx[h, s, :, rows] = jnp.maximum(
                        mx[h, s, :, rows],
                        jnp.max(scores.reshape(BLOCK // 8, 8, HALF), axis=0),
                    )

    for step in range(1, 4):
        x_copy(step).wait_recv()
    lens[1, z] = lens[0, 0] + lens[0, 1] + lens[0, 2] + lens[0, 3]
    for step in range(1, 4):
        z_copy(step).start()

    pair[3].wait_recv()
    pair[4].wait_recv()
    stage_do(1)
    stage_own(1)

    for h in range(HEADS):
        for s in range(2):
            top = jnp.max(mx[h, s], axis=0, keepdims=True) * EXP2
            mx[h, s] = jnp.broadcast_to(top, (8, CHUNK))
            for part in range(CHUNK // HALF):
                rows = pl.ds(part * HALF, HALF)
                power = jnp.exp2(own_scores(h, s, part) * EXP2 - mx[h, s, 0:1, rows]).astype(bf16)
                eo[h, s, :, rows] = power
                acc[h, s, :, rows] = dot(vot[h, s], power)

    @pl.loop(0, NBLOCK)
    def _(j):
        base = pl.multiple_of(j * BLOCK, BLOCK)
        vals = vbuf.at[pl.ds(base, BLOCK)]
        pltpu.make_async_copy(vals, vals, v_recv.at[j]).wait()

        @pl.when(j == 0)
        def _():
            for copy in passing(vbuf, v_send, v_recv):
                copy.start()

        for h in range(HEADS):
            cols = pl.ds(h * HD, HD)
            for n in range(BLOCK // 128):
                vt[h, 0:HD, pl.ds(base + n * 128, 128)] = vbuf[
                    pl.ds(base + n * 128, 128), cols
                ].T
            for s in range(2):
                for part in range(CHUNK // HALF):
                    rows = pl.ds(part * HALF, HALF)
                    scores = dot(kbuf[pl.ds(base, BLOCK), cols], qt[h, s, :, rows])
                    power = jnp.exp2(scores * EXP2 - mx[h, s, 0:1, rows]).astype(bf16)
                    e[h, j, s, :, rows] = power
                    acc[h, s, :, rows] += dot(vt[h, :, pl.ds(base, BLOCK)], power)

    for step in range(1, 4):
        z_copy(step).wait_recv()
    lens[2, rest] = lens[1, 0] + lens[1, 1] + lens[1, 2] + lens[1, 3]
    for step in range(1, 4):
        rest_copy(step).start()

    def put(src, out, dst_cols, n):
        return (
            pltpu.make_async_copy(src.at[0], out.at[0, :, dst_cols], out_sem.at[n]),
            send(src.at[1], out.at[0, :, dst_cols], out_send.at[n], out_recv.at[n], sibling),
        )

    for s in range(2):
        for h in range(HEADS):
            inv = 1.0 / acc[h, s, HD : HD + 1, :]
            acc[h, s, HD : HD + 1, :] = inv
            cotangent = dot_[h, s].astype(f32)
            total = jnp.sum(acc[h, s, 0:HD, :] * cotangent, axis=0, keepdims=True)
            cen[h, s] = total * inv * inv
            scaled = (cotangent * inv).astype(bf16)
            dot_[h, s] = scaled
            for g in range(GROUP):
                rows = slice(g * ROWS, (g + 1) * ROWS)
                don[h, s, rows, :] = scaled[:, rows].T

    half_rows = BLOCK // 2

    def grad_copy(j, half, n):
        dist = (1 - j) * (1 - 2 * half)
        slot = (y_hi * 2 + core) * 6 + lax.rem(dist + 3, 3) * 2 + y_lo
        to_y = lax.rem(y + n, 4)
        row = pl.multiple_of(j * BLOCK + half * half_rows + to_y * LOCAL, LOCAL)
        return send(
            dkv.at[pl.ds(row, LOCAL)],
            rkv.at[slot],
            grad_send.at[0],
            grad_recv,
            at(lax.rem(z + dist + 4, 4), to_y, half),
        )

    def far_copy(half):
        row = pl.multiple_of(3 * BLOCK + half * half_rows, half_rows)
        return send(
            dkv.at[pl.ds(row, half_rows)],
            far.at[half],
            grad_send.at[1 + half],
            far_recv.at[half],
            at(lax.rem(z + 1 + 2 * half, 4), y, core),
        )


    for h in range(HEADS):
        for s in range(2):
            dq[h, s] = jnp.zeros((HD, CHUNK), f32)

    @pl.loop(0, 2 * NBLOCK)
    def _(step):
        turn = step // 2
        middle = turn * (3 - turn) // 2
        j = (1 - middle) * (3 - turn) + middle * (2 - lax.rem(step, 2))
        half = lax.rem(step + turn * (2 - turn) * (3 - turn) // 2, 2)
        base = pl.multiple_of(j * BLOCK + half * half_rows, half_rows)
        inner = pl.ds(pl.multiple_of(half * half_rows, half_rows), half_rows)
        rows = pl.ds(base, half_rows)
        for h in range(HEADS):
            cols = pl.ds(h * HD, HD)
            dv_part = None
            dk_part = None
            for s in range(2):
                power = e[h, j, s, inner]
                grad = dot(vbuf[rows, cols], dot_[h, s])
                score = (power.astype(f32) * (grad - cen[h, s])).astype(bf16)
                dv_now = dot(power, don[h, s])
                dk_now = dot(score, qn[h, s])
                dv_part = dv_now if s == 0 else dv_part + dv_now
                dk_part = dk_now if s == 0 else dk_part + dk_now
                dq[h, s] += dot(kt[h, :, pl.ds(base, half_rows)], score)
            dkv[rows, pl.ds(h * HD, HD)] = dk_part.astype(bf16)
            dkv[rows, pl.ds(KCOLS + h * HD, HD)] = dv_part.astype(bf16)

        @pl.when(turn == 0)
        def _():
            far_copy(half).start()

        @pl.when(turn == 3)
        def _():
            pltpu.make_async_copy(far.at[half], far.at[half], far_recv.at[half]).wait()
            dkv[rows] = (dkv[rows].astype(f32) + far[half].astype(f32)).astype(bf16)

        @pl.when(turn > 0)
        def _():
            for n in range(4):

                if n == 0:

                    @pl.when(jnp.logical_or(j != 1, half != core))
                    def _():
                        grad_copy(j, half, 0).start()
                else:
                    grad_copy(j, half, n).start()

    pltpu.make_async_copy(
        dkv.at[pl.ds(BLOCK + my_row, LOCAL)], rkv.at[(y_hi * 2 + core) * 6 + y_lo], grad_recv
    ).start()

    for s in range(2):
        live = slot_row < lsum[s, 0:1, :]
        for h in range(HEADS):
            attended = acc[h, s, 0:HD, :] * acc[h, s, HD : HD + 1, :]
            for g in range(GROUP):
                rows = slice(g * ROWS, (g + 1) * ROWS)
                ost[s, :, pl.ds((h * GROUP + g) * HD, HD)] = jnp.where(
                    live, attended[:, rows].T, 0.0
                ).astype(bf16)
    o_copies = put(ost, o_out, my_q, 0)
    o_copies[0].start()
    o_copies[1].start()

    for step in range(1, 4):
        rest_copy(step).wait_recv()
    total = lens[2, 0] + lens[2, 1] + lens[2, 2] + lens[2, 3]
    weight = (4.0 * 16.0 * ROWS) / total[0:1, :]

    for h in range(HEADS):
        cols = pl.ds(h * HD, HD)
        for s in range(2):
            power = eo[h, s]
            grad = dot(vown[s, :, cols], dot_[h, s])
            score = (power.astype(f32) * (grad - cen[h, s])).astype(bf16)
            dvst[s, :, cols] = (dot(power, don[h, s]) * weight).astype(bf16)
            dkst[s, :, cols] = (dot(score, qn[h, s]) * (weight * FACTOR)).astype(bf16)
            dq[h, s] += dot(kot[h, s], score)
    dk_copies = put(dkst, dk_out, my_k, 1)
    dv_copies = put(dvst, dv_out, my_k, 2)
    for copy in dk_copies + dv_copies:
        copy.start()

    for s in range(2):
        for h in range(HEADS):
            for g in range(GROUP):
                rows = slice(g * ROWS, (g + 1) * ROWS)
                dqst[s, :, pl.ds((h * GROUP + g) * HD, HD)] = (
                    dq[h, s, :, rows].T * (weight * FACTOR)
                ).astype(bf16)
    dq_copies = put(dqst, dq_out, my_q, 3)
    for copy in dq_copies:
        copy.start()

    push_done(kbuf, k_send, k_recv)
    push_done(vbuf, v_send, v_recv)
    for copy in pair:
        copy.wait_send()
    for step in range(1, 4):
        x_copy(step).wait_send()
        z_copy(step).wait_send()
        rest_copy(step).wait_send()
    for half in range(2):
        far_copy(half).wait_send()
    for local, remote in (o_copies, dk_copies, dv_copies):
        local.wait()
        remote.wait_send()
        remote.wait_recv()
    sent = dkv.at[pl.ds(0, 23 * LOCAL)]
    pltpu.make_async_copy(sent, sent, grad_send.at[0]).wait()

    pltpu.make_async_copy(rkv, rkv, grad_recv).wait()
    twice = jnp.concatenate([weight, weight], axis=1)
    for n in range(4):
        summed = rkv[n * 6].astype(f32)
        for m in range(1, 6):
            summed += rkv[n * 6 + m].astype(f32)
        cols = slice(n * KCOLS, (n + 1) * KCOLS)
        pkg_out[0, :, cols] = (summed[:, :KCOLS] * (twice * FACTOR)).astype(bf16)
        pvg_out[0, :, cols] = (summed[:, KCOLS:] * twice).astype(bf16)
    dq_copies[0].wait()
    dq_copies[1].wait_send()
    dq_copies[1].wait_recv()


def copy_kernel(*refs):
    sources, results, held, (come, go) = refs[:6], refs[6:12], refs[12:18], refs[18:]
    loads = [pltpu.make_async_copy(sources[n], held[n], come.at[n]) for n in range(6)]
    stores = [pltpu.make_async_copy(held[n], results[n], go.at[n]) for n in range(6)]
    for copy in loads:
        copy.start()
    for n in range(6):
        loads[n].wait()
        stores[n].start()
    for copy in stores:
        copy.wait()


def body(queries, keys, values, prefix_keys, prefix_values, lengths, out_grad):
    vmem = lambda shape, dtype: pltpu.VMEM(shape, dtype)
    dma = pltpu.SemaphoreType.DMA
    prefix = NBLOCK * BLOCK
    anywhere = pl.BlockSpec(memory_space=pl.ANY)
    in_vmem = pl.BlockSpec(memory_space=pltpu.VMEM)
    shape = lambda a: jax.ShapeDtypeStruct(a.shape, bf16)
    results = pl.pallas_call(
        kernel,
        out_shape=[
            shape(queries), shape(queries), shape(keys), shape(values),
            shape(prefix_keys), shape(prefix_values),
        ],
        in_specs=[anywhere] * 5 + [pl.BlockSpec(memory_space=pltpu.SMEM), anywhere],
        out_specs=[anywhere] * 4 + [in_vmem] * 2,
        scratch_shapes=[
            vmem((LOCAL, 8 * HD), bf16), vmem((LOCAL, 8 * HD), bf16),
            vmem((2, ROWS, QCOLS), bf16), vmem((2, ROWS, QCOLS), bf16),
            vmem((2, ROWS, KCOLS), bf16), vmem((2, ROWS, KCOLS), bf16),
            vmem((prefix, KCOLS), bf16), vmem((prefix, KCOLS), bf16),
            vmem((3, 4, 8, 128), f32), vmem((2, 8, 128), f32),
            vmem((HEADS, 2, HD, CHUNK), bf16), vmem((HEADS, 2, CHUNK, HD), bf16),
            vmem((HEADS, 2, HD, CHUNK), bf16), vmem((HEADS, 2, CHUNK, HD), bf16),
            vmem((HEADS, HD + 16, prefix), bf16), vmem((HEADS, HD, prefix), bf16),
            vmem((HEADS, 2, HD, ROWS), bf16), vmem((HEADS, 2, HD + 16, ROWS), bf16),
            vmem((HEADS, NBLOCK, 2, BLOCK, CHUNK), bf16),
            vmem((HEADS, 2, ROWS, CHUNK), bf16),
            vmem((HEADS, 2, 8, CHUNK), f32),
            vmem((HEADS, 2, HD + 16, CHUNK), f32),
            vmem((HEADS, 2, 1, CHUNK), f32),
            vmem((HEADS, 2, HD, CHUNK), f32),
            vmem((2, ROWS, QCOLS), bf16), vmem((2, ROWS, QCOLS), bf16),
            vmem((2, ROWS, KCOLS), bf16), vmem((2, ROWS, KCOLS), bf16),
            vmem((prefix, 2 * KCOLS), bf16),
            vmem((24, LOCAL, 2 * KCOLS), bf16),
            vmem((2, BLOCK // 2, 2 * KCOLS), bf16),
            dma((6,)), dma((5,)), dma((5,)),
            dma((3,)), dma((3,)), dma((NBLOCK,)), dma((NBLOCK,)),
            dma((3, 3)), dma((3, 3)),
            dma((3,)), dma, dma((2,)),
            dma((4,)), dma((4,)), dma((4,)),
        ],
        compiler_params=pltpu.CompilerParams(
            collective_id=0, has_side_effects=True, vmem_limit_bytes=60 * 2**20
        ),
        cost_estimate=pl.CostEstimate(
            flops=14 * 2**30, bytes_accessed=10 * 2**20, transcendentals=9 * 2**20
        ),
    )(queries, keys, values, prefix_keys, prefix_values, lengths, out_grad)
    return pl.pallas_call(
        copy_kernel,
        out_shape=[jax.ShapeDtypeStruct(a.shape, a.dtype) for a in results],
        in_specs=[anywhere] * 6,
        out_specs=[anywhere] * 6,
        scratch_shapes=[vmem(a.shape, a.dtype) for a in results] + [dma((6,)), dma((6,))],
    )(*results)


def solution(mesh):
    in_specs = (
        P("prompt", "response", "tensor"),
        P("prompt", "response", "tensor"),
        P("prompt", "response", "tensor"),
        P("prompt", ("response", "tensor"), None),
        P("prompt", ("response", "tensor"), None),
        P("prompt", "response"),
        P("prompt", "response", "tensor"),
    )
    out_specs = (
        P("prompt", "response", "tensor"),
        P("prompt", "response", "tensor"),
        P("prompt", "response", "tensor"),
        P("prompt", "response", "tensor"),
        P("prompt", ("response", "tensor"), None),
        P("prompt", ("response", "tensor"), None),
    )
    return jax.shard_map(body, mesh=mesh, in_specs=in_specs, out_specs=out_specs, check_vma=False)
```

```python
import math

import jax
import jax.numpy as jnp
from jax import lax
from jax.experimental import pallas as pl
from jax.experimental.pallas import tpu as pltpu
from jax.sharding import PartitionSpec as P

HD = 128
GROUP = 8
ROWS = 128
LOCAL = 64
BLOCK = 512
NBLOCK = 4
CHUNK = 1024
HALF = 1024
HEADS = 2
QCOLS = HEADS * GROUP * HD
KCOLS = HEADS * HD
FACTOR = 1.0 / math.sqrt(HD)
EXP2 = math.log2(math.e) * FACTOR
MESH = pl.DeviceIdType.MESH
f32 = jnp.float32
bf16 = jnp.bfloat16


def dot(a, b):
    return jnp.dot(a, b, preferred_element_type=f32)


def kernel(
    q_in, k_in, v_in, pk_in, pv_in, len_in, do_in,
    o_out, dq_out, dk_out, dv_out, pkg_out, pvg_out,
    pk, pv, qin, din, kown, vown, kbuf, vbuf, lens, lsum,
    qt, qn, dot_, don, vt, kt, kot, vot, e, eo, mx, acc, cen, dq,
    ost, dqst, dkst, dvst, dkv, rkv, far,
    load_sem, pair_send, pair_recv, k_send, v_send, k_recv, v_recv,
    len_send, len_recv, grad_send, grad_recv, far_recv, out_send, out_recv, out_sem,
):
    prompt = lax.axis_index("prompt")
    resp = lax.axis_index("response")
    y_hi = lax.axis_index("tensor")
    core = lax.rem(resp, 2)
    z = lax.rem(resp // 2, 4)
    y_lo = resp // 8
    y = y_hi * 2 + y_lo
    other = 1 - core

    def at(zz, yy, cc):
        return {"response": lax.rem(yy, 2) * 8 + zz * 2 + cc, "tensor": yy // 2}

    def along_x(pp):
        return {"prompt": pp}

    sibling = {"response": resp + 1 - 2 * core}
    my_q = pl.ds(pl.multiple_of(core * QCOLS, QCOLS), QCOLS)
    its_q = pl.ds(pl.multiple_of(other * QCOLS, QCOLS), QCOLS)
    my_k = pl.ds(pl.multiple_of(core * KCOLS, KCOLS), KCOLS)
    its_k = pl.ds(pl.multiple_of(other * KCOLS, KCOLS), KCOLS)

    loads = [
        pltpu.make_async_copy(pk_in.at[0], pk, load_sem.at[0]),
        pltpu.make_async_copy(pv_in.at[0], pv, load_sem.at[1]),
        pltpu.make_async_copy(q_in.at[0, :, my_q], qin.at[0], load_sem.at[2]),
        pltpu.make_async_copy(do_in.at[0, :, my_q], din.at[0], load_sem.at[3]),
        pltpu.make_async_copy(k_in.at[0, :, my_k], kown.at[0], load_sem.at[4]),
        pltpu.make_async_copy(v_in.at[0, :, my_k], vown.at[0], load_sem.at[5]),
    ]
    for copy in loads:
        copy.start()

    barrier = pltpu.get_barrier_semaphore()

    def greet(device):
        pl.semaphore_signal(barrier, inc=1, device_id=device, device_id_type=MESH)

    for dist in (1, 3, 0):
        for n in range(8):
            if dist or n:
                greet(
                    at(
                        lax.rem(z + dist, 4),
                        lax.rem(y + n // 2, 4),
                        lax.rem(core + n % 2, 2),
                    )
                )
    greet(at(lax.rem(z + 2, 4), y, core))
    for step in range(1, 4):
        greet(along_x(lax.rem(prompt + step, 4)))
    pl.semaphore_wait(barrier, 27)

    def send(src, dst, send_sem, recv_sem, device):
        return pltpu.make_async_remote_copy(
            src_ref=src,
            dst_ref=dst,
            send_sem=send_sem,
            recv_sem=recv_sem,
            device_id=device,
            device_id_type=MESH,
        )

    lens[0, prompt] = jnp.full((8, 128), len_in[0, 0], jnp.int32).astype(f32)
    pair = [
        send(lens.at[0, prompt], lsum.at[1], pair_send.at[0], pair_recv.at[0], sibling),
        send(q_in.at[0, :, its_q], qin.at[1], pair_send.at[1], pair_recv.at[1], sibling),
        send(k_in.at[0, :, its_k], kown.at[1], pair_send.at[2], pair_recv.at[2], sibling),
        send(do_in.at[0, :, its_q], din.at[1], pair_send.at[3], pair_recv.at[3], sibling),
        send(v_in.at[0, :, its_k], vown.at[1], pair_send.at[4], pair_recv.at[4], sibling),
    ]
    lsum[0] = lens[0, prompt]
    pair[0].start()
    pair[1].start()
    pair[2].start()

    my_row = pl.multiple_of((core * 4 + y) * LOCAL, LOCAL)
    up, down = lax.rem(z + 1, 4), lax.rem(z + 3, 4)
    routes = ((0, lax.rem(z + 3 + 2 * core, 4)), (1, z), (2, lax.rem(z + 5 - 2 * core, 4)))

    def push(shard, buf, send_sems, recv_sems):
        for block, to_z in routes:
            for n in range(8):
                if block == 1 and n == 0:
                    continue
                to_y = lax.rem(y + n // 2, 4)
                to_core = lax.rem(core + n % 2, 2)
                cols = pl.multiple_of(((to_y // 2) * 2 + to_core) * KCOLS, KCOLS)
                send(
                    shard.at[:, pl.ds(cols, KCOLS)],
                    buf.at[pl.ds(block * BLOCK + my_row, LOCAL)],
                    send_sems.at[0],
                    recv_sems.at[block],
                    at(to_z, to_y, to_core),
                ).start()

    def passing(buf, send_sems, recv_sems):
        half = BLOCK // 2
        return [
            send(
                buf.at[pl.ds(n * half, half)],
                buf.at[pl.ds(3 * BLOCK + n * half, half)],
                send_sems.at[1 + n],
                recv_sems.at[3],
                at(down if n == 0 else up, y, core),
            )
            for n in range(2)
        ]

    def push_done(buf, send_sems, recv_sems):
        sent = buf.at[pl.ds(0, 23 * LOCAL)]
        pltpu.make_async_copy(sent, sent, send_sems.at[0]).wait()
        for copy in passing(buf, send_sems, recv_sems):
            copy.wait_send()

    mine = pl.ds(pl.multiple_of((y_hi * 2 + core) * KCOLS, KCOLS), KCOLS)
    loads[0].wait()
    push(pk, kbuf, k_send, k_recv)
    pltpu.make_async_copy(pk.at[:, mine], kbuf.at[pl.ds(BLOCK + my_row, LOCAL)], k_recv.at[1]).start()
    pair[3].start()
    pair[4].start()
    loads[1].wait()
    pltpu.make_async_copy(pv.at[:, mine], vbuf.at[pl.ds(BLOCK + my_row, LOCAL)], v_recv.at[1]).start()

    def x_copy(step):
        return send(
            lens.at[0, prompt], lens.at[0, prompt], len_send.at[0, step - 1],
            len_recv.at[0, step - 1], along_x(lax.rem(prompt + step, 4)),
        )

    def z_copy(step):
        return send(
            lens.at[1, z], lens.at[1, z], len_send.at[1, step - 1],
            len_recv.at[1, step - 1], at(lax.rem(z + step, 4), y, core),
        )

    rest = y_lo * 2 + core

    def rest_copy(step):
        slot = lax.rem(rest + step, 4)
        return send(
            lens.at[2, rest], lens.at[2, rest], len_send.at[2, step - 1],
            len_recv.at[2, step - 1], at(z, y_hi * 2 + slot // 2, lax.rem(slot, 2)),
        )

    for step in range(1, 4):
        x_copy(step).start()

    slot_row = lax.broadcasted_iota(jnp.int32, (ROWS, HD), 0).astype(f32)

    def stage_q(s):
        for h in range(HEADS):
            for g in range(GROUP):
                cols = pl.ds((h * GROUP + g) * HD, HD)
                block = qin[s, :, cols]
                qn[h, s, g * ROWS : (g + 1) * ROWS, :] = block
                qt[h, s, :, g * ROWS : (g + 1) * ROWS] = block.T

    def stage_do(s):
        live = slot_row < lsum[s, 0:1, :]
        for h in range(HEADS):
            for g in range(GROUP):
                cols = pl.ds((h * GROUP + g) * HD, HD)
                block = jnp.where(live, din[s, :, cols].astype(f32), 0.0).astype(bf16)
                dot_[h, s, :, g * ROWS : (g + 1) * ROWS] = block.T

    def stage_own(s):
        for h in range(HEADS):
            cols = pl.ds(h * HD, HD)
            kot[h, s] = kown[s, :, cols].T
            vot[h, s, 0:HD] = vown[s, :, cols].T
            vot[h, s, HD : HD + 16] = jnp.ones((16, ROWS), bf16)

    allowed = lax.broadcasted_iota(jnp.int32, (ROWS, HALF), 0) <= lax.rem(
        lax.broadcasted_iota(jnp.int32, (ROWS, HALF), 1), ROWS
    )

    def own_scores(h, s, part):
        scores = dot(kown[s, :, pl.ds(h * HD, HD)], qt[h, s, :, part * HALF : (part + 1) * HALF])
        return jnp.where(allowed, scores, -1e30)

    def own_max(s):
        for h in range(HEADS):
            for part in range(CHUNK // HALF):
                cols = pl.ds(part * HALF, HALF)
                mx[h, s, :, cols] = jnp.max(
                    own_scores(h, s, part).reshape(ROWS // 8, 8, HALF), axis=0
                )

    loads[2].wait()
    loads[4].wait()
    stage_q(0)
    own_max(0)
    loads[3].wait()
    stage_do(0)
    loads[5].wait()
    stage_own(0)
    for h in range(HEADS):
        vt[h, HD : HD + 16] = jnp.ones((16, NBLOCK * BLOCK), bf16)
    pair[0].wait_recv()
    pair[1].wait_recv()
    pair[2].wait_recv()
    stage_q(1)
    own_max(1)

    push(pv, vbuf, v_send, v_recv)
    @pl.loop(0, NBLOCK)
    def _(j):
        base = pl.multiple_of(j * BLOCK, BLOCK)
        keys = kbuf.at[pl.ds(base, BLOCK)]
        pltpu.make_async_copy(keys, keys, k_recv.at[j]).wait()

        @pl.when(j == 0)
        def _():
            for copy in passing(kbuf, k_send, k_recv):
                copy.start()

        for h in range(HEADS):
            cols = pl.ds(h * HD, HD)
            for n in range(BLOCK // 128):
                kt[h, :, pl.ds(base + n * 128, 128)] = kbuf[pl.ds(base + n * 128, 128), cols].T
            for s in range(2):
                for part in range(CHUNK // HALF):
                    rows = pl.ds(part * HALF, HALF)
                    scores = dot(kbuf[pl.ds(base, BLOCK), cols], qt[h, s, :, rows])
                    mx[h, s, :, rows] = jnp.maximum(
                        mx[h, s, :, rows],
                        jnp.max(scores.reshape(BLOCK // 8, 8, HALF), axis=0),
                    )

    for step in range(1, 4):
        x_copy(step).wait_recv()
    lens[1, z] = lens[0, 0] + lens[0, 1] + lens[0, 2] + lens[0, 3]
    for step in range(1, 4):
        z_copy(step).start()

    pair[3].wait_recv()
    pair[4].wait_recv()
    stage_do(1)
    stage_own(1)

    for h in range(HEADS):
        for s in range(2):
            top = jnp.max(mx[h, s], axis=0, keepdims=True) * EXP2
            mx[h, s] = jnp.broadcast_to(top, (8, CHUNK))
            for part in range(CHUNK // HALF):
                rows = pl.ds(part * HALF, HALF)
                power = jnp.exp2(own_scores(h, s, part) * EXP2 - mx[h, s, 0:1, rows]).astype(bf16)
                eo[h, s, :, rows] = power
                acc[h, s, :, rows] = dot(vot[h, s], power)

    @pl.loop(0, NBLOCK)
    def _(j):
        base = pl.multiple_of(j * BLOCK, BLOCK)
        vals = vbuf.at[pl.ds(base, BLOCK)]
        pltpu.make_async_copy(vals, vals, v_recv.at[j]).wait()

        @pl.when(j == 0)
        def _():
            for copy in passing(vbuf, v_send, v_recv):
                copy.start()

        for h in range(HEADS):
            cols = pl.ds(h * HD, HD)
            for n in range(BLOCK // 128):
                vt[h, 0:HD, pl.ds(base + n * 128, 128)] = vbuf[
                    pl.ds(base + n * 128, 128), cols
                ].T
            for s in range(2):
                for part in range(CHUNK // HALF):
                    rows = pl.ds(part * HALF, HALF)
                    scores = dot(kbuf[pl.ds(base, BLOCK), cols], qt[h, s, :, rows])
                    power = jnp.exp2(scores * EXP2 - mx[h, s, 0:1, rows]).astype(bf16)
                    e[h, j, s, :, rows] = power
                    acc[h, s, :, rows] += dot(vt[h, :, pl.ds(base, BLOCK)], power)

    for step in range(1, 4):
        z_copy(step).wait_recv()
    lens[2, rest] = lens[1, 0] + lens[1, 1] + lens[1, 2] + lens[1, 3]
    for step in range(1, 4):
        rest_copy(step).start()

    def put(src, out, dst_cols, n):
        return (
            pltpu.make_async_copy(src.at[0], out.at[0, :, dst_cols], out_sem.at[n]),
            send(src.at[1], out.at[0, :, dst_cols], out_send.at[n], out_recv.at[n], sibling),
        )

    for s in range(2):
        for h in range(HEADS):
            inv = 1.0 / acc[h, s, HD : HD + 1, :]
            acc[h, s, HD : HD + 1, :] = inv
            cotangent = dot_[h, s].astype(f32)
            total = jnp.sum(acc[h, s, 0:HD, :] * cotangent, axis=0, keepdims=True)
            cen[h, s] = total * inv * inv
            scaled = (cotangent * inv).astype(bf16)
            dot_[h, s] = scaled
            for g in range(GROUP):
                rows = slice(g * ROWS, (g + 1) * ROWS)
                don[h, s, rows, :] = scaled[:, rows].T

    half_rows = BLOCK // 2

    def grad_copy(j, half, n):
        dist = (1 - j) * (1 - 2 * half)
        slot = (y_hi * 2 + core) * 6 + lax.rem(dist + 3, 3) * 2 + y_lo
        to_y = lax.rem(y + n, 4)
        row = pl.multiple_of(j * BLOCK + half * half_rows + to_y * LOCAL, LOCAL)
        return send(
            dkv.at[pl.ds(row, LOCAL)],
            rkv.at[slot],
            grad_send.at[0],
            grad_recv,
            at(lax.rem(z + dist + 4, 4), to_y, half),
        )

    def far_copy(half):
        row = pl.multiple_of(3 * BLOCK + half * half_rows, half_rows)
        return send(
            dkv.at[pl.ds(row, half_rows)],
            far.at[half],
            grad_send.at[1 + half],
            far_recv.at[half],
            at(lax.rem(z + 1 + 2 * half, 4), y, core),
        )


    for h in range(HEADS):
        for s in range(2):
            dq[h, s] = jnp.zeros((HD, CHUNK), f32)

    @pl.loop(0, 2 * NBLOCK)
    def _(step):
        turn = step // 2
        middle = turn * (3 - turn) // 2
        j = (1 - middle) * (3 - turn) + middle * (2 - lax.rem(step, 2))
        half = lax.rem(step + turn * (2 - turn) * (3 - turn) // 2, 2)
        base = pl.multiple_of(j * BLOCK + half * half_rows, half_rows)
        inner = pl.ds(pl.multiple_of(half * half_rows, half_rows), half_rows)
        rows = pl.ds(base, half_rows)
        for h in range(HEADS):
            cols = pl.ds(h * HD, HD)
            dv_part = None
            dk_part = None
            for s in range(2):
                power = e[h, j, s, inner]
                grad = dot(vbuf[rows, cols], dot_[h, s])
                score = (power.astype(f32) * (grad - cen[h, s])).astype(bf16)
                dv_now = dot(power, don[h, s])
                dk_now = dot(score, qn[h, s])
                dv_part = dv_now if s == 0 else dv_part + dv_now
                dk_part = dk_now if s == 0 else dk_part + dk_now
                dq[h, s] += dot(kt[h, :, pl.ds(base, half_rows)], score)
            dkv[rows, pl.ds(h * HD, HD)] = dk_part.astype(bf16)
            dkv[rows, pl.ds(KCOLS + h * HD, HD)] = dv_part.astype(bf16)

        @pl.when(turn == 0)
        def _():
            far_copy(half).start()

        @pl.when(turn == 3)
        def _():
            pltpu.make_async_copy(far.at[half], far.at[half], far_recv.at[half]).wait()
            dkv[rows] = (dkv[rows].astype(f32) + far[half].astype(f32)).astype(bf16)

        @pl.when(turn > 0)
        def _():
            for n in range(4):

                if n == 0:

                    @pl.when(jnp.logical_or(j != 1, half != core))
                    def _():
                        grad_copy(j, half, 0).start()
                else:
                    grad_copy(j, half, n).start()

    pltpu.make_async_copy(
        dkv.at[pl.ds(BLOCK + my_row, LOCAL)], rkv.at[(y_hi * 2 + core) * 6 + y_lo], grad_recv
    ).start()

    for s in range(2):
        live = slot_row < lsum[s, 0:1, :]
        for h in range(HEADS):
            attended = acc[h, s, 0:HD, :] * acc[h, s, HD : HD + 1, :]
            for g in range(GROUP):
                rows = slice(g * ROWS, (g + 1) * ROWS)
                ost[s, :, pl.ds((h * GROUP + g) * HD, HD)] = jnp.where(
                    live, attended[:, rows].T, 0.0
                ).astype(bf16)
    o_copies = put(ost, o_out, my_q, 0)
    o_copies[0].start()
    o_copies[1].start()

    for step in range(1, 4):
        rest_copy(step).wait_recv()
    total = lens[2, 0] + lens[2, 1] + lens[2, 2] + lens[2, 3]
    weight = (4.0 * 16.0 * ROWS) / total[0:1, :]

    for h in range(HEADS):
        cols = pl.ds(h * HD, HD)
        for s in range(2):
            power = eo[h, s]
            grad = dot(vown[s, :, cols], dot_[h, s])
            score = (power.astype(f32) * (grad - cen[h, s])).astype(bf16)
            dvst[s, :, cols] = (dot(power, don[h, s]) * weight).astype(bf16)
            dkst[s, :, cols] = (dot(score, qn[h, s]) * (weight * FACTOR)).astype(bf16)
            dq[h, s] += dot(kot[h, s], score)
    dk_copies = put(dkst, dk_out, my_k, 1)
    dv_copies = put(dvst, dv_out, my_k, 2)
    for copy in dk_copies + dv_copies:
        copy.start()

    for s in range(2):
        for h in range(HEADS):
            for g in range(GROUP):
                rows = slice(g * ROWS, (g + 1) * ROWS)
                dqst[s, :, pl.ds((h * GROUP + g) * HD, HD)] = (
                    dq[h, s, :, rows].T * (weight * FACTOR)
                ).astype(bf16)
    dq_copies = put(dqst, dq_out, my_q, 3)
    for copy in dq_copies:
        copy.start()

    push_done(kbuf, k_send, k_recv)
    push_done(vbuf, v_send, v_recv)
    for copy in pair:
        copy.wait_send()
    for step in range(1, 4):
        x_copy(step).wait_send()
        z_copy(step).wait_send()
        rest_copy(step).wait_send()
    for half in range(2):
        far_copy(half).wait_send()
    for local, remote in (o_copies, dk_copies, dv_copies):
        local.wait()
        remote.wait_send()
        remote.wait_recv()
    sent = dkv.at[pl.ds(0, 23 * LOCAL)]
    pltpu.make_async_copy(sent, sent, grad_send.at[0]).wait()

    pltpu.make_async_copy(rkv, rkv, grad_recv).wait()
    twice = jnp.concatenate([weight, weight], axis=1)
    for n in range(4):
        summed = rkv[n * 6].astype(f32)
        for m in range(1, 6):
            summed += rkv[n * 6 + m].astype(f32)
        cols = slice(n * KCOLS, (n + 1) * KCOLS)
        pkg_out[0, :, cols] = (summed[:, :KCOLS] * (twice * FACTOR)).astype(bf16)
        pvg_out[0, :, cols] = (summed[:, KCOLS:] * twice).astype(bf16)
    dq_copies[0].wait()
    dq_copies[1].wait_send()
    dq_copies[1].wait_recv()


def copy_kernel(*refs):
    sources, results, held, (come, go) = refs[:6], refs[6:12], refs[12:18], refs[18:]
    parts = [(n, pl.ds(32 * m, 32)) for n in (0, 1) for m in range(4)]
    parts += [(n, slice(None)) for n in range(2, 6)]
    loads, stores = [], []
    for k, (n, rows) in enumerate(parts):
        block = held[n].at[:, rows]
        loads.append(pltpu.make_async_copy(sources[n].at[:, rows], block, come.at[k]))
        stores.append(pltpu.make_async_copy(block, results[n].at[:, rows], go.at[k]))
    for copy in loads:
        copy.start()
    for load, store in zip(loads, stores):
        load.wait()
        store.start()
    for copy in stores:
        copy.wait()


def body(queries, keys, values, prefix_keys, prefix_values, lengths, out_grad):
    vmem = lambda shape, dtype: pltpu.VMEM(shape, dtype)
    dma = pltpu.SemaphoreType.DMA
    prefix = NBLOCK * BLOCK
    anywhere = pl.BlockSpec(memory_space=pl.ANY)
    in_vmem = pl.BlockSpec(memory_space=pltpu.VMEM)
    shape = lambda a: jax.ShapeDtypeStruct(a.shape, bf16)
    results = pl.pallas_call(
        kernel,
        out_shape=[
            shape(queries), shape(queries), shape(keys), shape(values),
            shape(prefix_keys), shape(prefix_values),
        ],
        in_specs=[anywhere] * 5 + [pl.BlockSpec(memory_space=pltpu.SMEM), anywhere],
        out_specs=[anywhere] * 4 + [in_vmem] * 2,
        scratch_shapes=[
            vmem((LOCAL, 8 * HD), bf16), vmem((LOCAL, 8 * HD), bf16),
            vmem((2, ROWS, QCOLS), bf16), vmem((2, ROWS, QCOLS), bf16),
            vmem((2, ROWS, KCOLS), bf16), vmem((2, ROWS, KCOLS), bf16),
            vmem((prefix, KCOLS), bf16), vmem((prefix, KCOLS), bf16),
            vmem((3, 4, 8, 128), f32), vmem((2, 8, 128), f32),
            vmem((HEADS, 2, HD, CHUNK), bf16), vmem((HEADS, 2, CHUNK, HD), bf16),
            vmem((HEADS, 2, HD, CHUNK), bf16), vmem((HEADS, 2, CHUNK, HD), bf16),
            vmem((HEADS, HD + 16, prefix), bf16), vmem((HEADS, HD, prefix), bf16),
            vmem((HEADS, 2, HD, ROWS), bf16), vmem((HEADS, 2, HD + 16, ROWS), bf16),
            vmem((HEADS, NBLOCK, 2, BLOCK, CHUNK), bf16),
            vmem((HEADS, 2, ROWS, CHUNK), bf16),
            vmem((HEADS, 2, 8, CHUNK), f32),
            vmem((HEADS, 2, HD + 16, CHUNK), f32),
            vmem((HEADS, 2, 1, CHUNK), f32),
            vmem((HEADS, 2, HD, CHUNK), f32),
            vmem((2, ROWS, QCOLS), bf16), vmem((2, ROWS, QCOLS), bf16),
            vmem((2, ROWS, KCOLS), bf16), vmem((2, ROWS, KCOLS), bf16),
            vmem((prefix, 2 * KCOLS), bf16),
            vmem((24, LOCAL, 2 * KCOLS), bf16),
            vmem((2, BLOCK // 2, 2 * KCOLS), bf16),
            dma((6,)), dma((5,)), dma((5,)),
            dma((3,)), dma((3,)), dma((NBLOCK,)), dma((NBLOCK,)),
            dma((3, 3)), dma((3, 3)),
            dma((3,)), dma, dma((2,)),
            dma((4,)), dma((4,)), dma((4,)),
        ],
        compiler_params=pltpu.CompilerParams(
            collective_id=0, has_side_effects=True, vmem_limit_bytes=60 * 2**20
        ),
        cost_estimate=pl.CostEstimate(
            flops=14 * 2**30, bytes_accessed=10 * 2**20, transcendentals=9 * 2**20
        ),
    )(queries, keys, values, prefix_keys, prefix_values, lengths, out_grad)
    return pl.pallas_call(
        copy_kernel,
        out_shape=[jax.ShapeDtypeStruct(a.shape, a.dtype) for a in results],
        in_specs=[anywhere] * 6,
        out_specs=[anywhere] * 6,
        scratch_shapes=[vmem(a.shape, a.dtype) for a in results] + [dma((12,)), dma((12,))],
    )(*results)


def solution(mesh):
    in_specs = (
        P("prompt", "response", "tensor"),
        P("prompt", "response", "tensor"),
        P("prompt", "response", "tensor"),
        P("prompt", ("response", "tensor"), None),
        P("prompt", ("response", "tensor"), None),
        P("prompt", "response"),
        P("prompt", "response", "tensor"),
    )
    out_specs = (
        P("prompt", "response", "tensor"),
        P("prompt", "response", "tensor"),
        P("prompt", "response", "tensor"),
        P("prompt", "response", "tensor"),
        P("prompt", ("response", "tensor"), None),
        P("prompt", ("response", "tensor"), None),
    )
    return jax.shard_map(body, mesh=mesh, in_specs=in_specs, out_specs=out_specs, check_vma=False)
```
